512 devices in a mesh: row: 16 (over x, y_hi, core), col: 32 (over z, y_lo).
Axes of the slice: x: 4, y: 8 (y_hi: 2, y_lo: 4; y = y_hi * 4 + y_lo), z: 8, core: 2. Of those that a mesh axis runs over, the one named last changes fastest.
Arguments:
- block_in: bfloat16 [1024, 6144], P('col', 'row'), may hold values from -6 to 6
- block_out: bfloat16 [1024, 6144], P('col', 'row'), may hold values from -40 to 40
- hidden_pre: bfloat16 [1024, 24576], P(None, 'col'), may hold values from -6 to 6
- w_in: bfloat16 [6144, 24576], P('row', 'col'), may hold values from -0.078125 to 0.078125
- w_out: bfloat16 [24576, 6144], P('col', 'row'), may hold values from -0.0390625 to 0.0390625
- phrases: bfloat16 [512, 6144], P(None, 'row'), may hold values from -0.078125 to 0.078125
- region_ids: int32 [1024], replicated, may hold values from 0 to 511, never falling along the last dimension, each value on 1 to 4 neighbouring positions
- positive_phrase: int32 [512], replicated, may hold values from 0 to 511
Outputs:
- grad_in: bfloat16 [1024, 6144], P('col', 'row')
- grad_w_in: bfloat16 [6144, 24576], P('row', 'col')
- grad_w_out: bfloat16 [24576, 6144], P('col', 'row')
The draws below stay inside these ranges and needn't reach their ends.
Inputs may be any that keep to these rules, and one draw needn't show every extreme that they name: `region_ids`: nondecreasing along the token dimension; each region holds 1 to 4 tokens.
All inputs are finite; a program needn't handle non-finite values.
Results may differ from the reference program's by a relative error of at most 0.007.
Values may be sent and summed in bfloat16 or wider, within the bound.
A program may use at most 64 MiB of HBM per device.

```python
import math
import jax
import jax.numpy as jnp
import numpy as np
from jax import lax

D = 6144
FF = 24576
TOKENS = 1024
REGIONS = 512
PHRASES = 512


def draw_block_out(key, part):
    key = jax.random.fold_in(key, 7)
    key_noise, key_rows = jax.random.split(key, 2)
    column_place = lax.broadcasted_iota(jnp.float32, (TOKENS, D), 1) / D
    column_scale = 10.0 ** (column_place - 0.5)
    row_scale = 10.0 ** (jax.random.uniform(key_rows, (TOKENS, 1), dtype=jnp.float32) - 0.5)
    base = jax.random.truncated_normal(key_noise, -4.0, 4.0, (TOKENS, D), dtype=jnp.float32)
    return (base * column_scale * row_scale).astype(jnp.bfloat16)


def place_ends(array, key, low, top_value):
    longest = array.shape.index(max(array.shape))
    spots = []
    for shift in (0, 1):
        where = [jax.random.randint(jax.random.fold_in(key, axis), (), 0, length) for axis, length in enumerate(array.shape)]
        where[longest] = (where[longest] + shift) % array.shape[longest]
        spots.append(tuple(where))
    return array.at[spots[0]].set(low).at[spots[1]].set(top_value)


def block_scale(stream_key, shape, shards, low, top_value):
    level = 1.0
    for position, blocks in shards:
        draws = jax.random.uniform(jax.random.fold_in(jax.random.fold_in(stream_key, 6), position), (blocks,), jnp.float32, low / len(shards), top_value / len(shards))
        level = level * jnp.repeat(jnp.exp(draws), shape[position] // blocks).reshape((-1,) + (1,) * (len(shape) - 1 - position))
    return level


def split_up(count, total, reach, lean):
    weights = [(1 << 20) // math.isqrt(rank ** lean) + 1 for rank in range(2, count + 1)]
    surplus, given = total - reach - (count - 1), [1] * (count - 1)
    while surplus > 0:
        movable = [i for i in range(count - 1) if given[i] < reach]
        whole, remaining = sum([weights[i] for i in movable]), surplus
        for i in movable:
            addition = min(reach - given[i], max(1, remaining * weights[i] // whole), surplus)
            given[i] = given[i] + addition
            surplus = surplus - addition
    return np.array([reach] + given)


def ragged(key, number_of, total, most, lean):
    if number_of == 2:
        one = jax.random.randint(key, (), max(1, total - most), min(most, total - 1) + 1)
        return jnp.stack([one, total - one])
    sizes = jnp.asarray(split_up(number_of, total, most, lean), jnp.int32)
    pairs = (number_of - 1) // 2
    source_of, sink = sizes[1:1 + 2 * pairs:2], sizes[2:2 + 2 * pairs:2]
    margin = jnp.minimum(source_of - 1, most - sink)
    passed = jax.random.randint(jax.random.fold_in(key, 1), (pairs,), 0, 1 << 20) % (margin + 1)
    sizes = sizes.at[1:1 + 2 * pairs:2].set(source_of - passed).at[2:2 + 2 * pairs:2].set(sink + passed)
    return sizes[jax.random.permutation(jax.random.fold_in(key, 2), number_of)]


def normal_values(own_key, shape, width, reach, pieces=(), kind=jnp.bfloat16):
    loudness = block_scale(own_key, shape, pieces, -0.22, 0.18) if pieces else 1.0
    result = jax.random.normal(own_key, shape, jnp.float32) * width * loudness
    return jnp.minimum(jnp.maximum(result, -reach), reach).astype(kind)


def setup_inputs(seed: int = 0) -> dict:
    key_list = jax.random.split(jax.random.key(seed), 9)
    return {
        "block_in": normal_values(key_list[0], (TOKENS, D), 1.0, 6.0, ((0, 32), (1, 16))),
        "block_out": draw_block_out(jax.random.fold_in(key_list[8], 71), 0),
        "hidden_pre": normal_values(key_list[2], (TOKENS, FF), 1.0, 6.0, ((1, 32),)),
        "w_in": normal_values(key_list[3], (D, FF), D ** -0.5, 0.078125, ((0, 16), (1, 32))),
        "w_out": normal_values(key_list[4], (FF, D), FF ** -0.5, 0.0390625, ((0, 32), (1, 16))),
        "phrases": normal_values(key_list[5], (PHRASES, D), D ** -0.5, 0.078125, ((1, 16),)),
        "region_ids": jnp.searchsorted(jnp.cumsum(ragged(key_list[6], REGIONS, TOKENS, 4, 0)), jnp.arange(TOKENS), side="right").astype(jnp.int32),
        "positive_phrase": place_ends(jax.random.randint(key_list[7], (REGIONS,), 0, PHRASES), jax.random.fold_in(key_list[7], 1), 0, PHRASES - 1).astype(jnp.int32),
    }


score_scale = 3.0
score_shift = -2.0
epsilon = 1e-06
half_root = 0.7071067811865476
density_norm = 0.3989422804014327

def gelu_slope(preact):
    return 0.5 * (1.0 + lax.erf(preact * half_root)) + preact * jnp.exp(-0.5 * preact * preact) * density_norm

def reference(block_in, block_out, hidden_pre, w_in, w_out, phrases, region_ids, positive_phrase):
    members = jnp.arange(REGIONS, dtype=jnp.int32)[:, None] == region_ids[None, :]
    counts = lax.optimization_barrier(jnp.sum(members.astype(jnp.float32), axis=1))
    pooled = jnp.dot(members.astype(jnp.bfloat16), block_out, preferred_element_type=jnp.float32) / counts[:, None]
    phrase_data = phrases.astype(jnp.float32)
    inner = jnp.dot(pooled, phrase_data.T, precision=lax.Precision.HIGHEST, preferred_element_type=jnp.float32)
    norms = jnp.sqrt(lax.optimization_barrier(jnp.mean(pooled * pooled, axis=1)) + epsilon)
    scores = inner / norms[:, None]
    labels = jnp.where(jnp.arange(PHRASES, dtype=jnp.int32)[None, :] == positive_phrase[:, None], jnp.float32(1.0), jnp.float32(-1.0))
    grad_scores = -labels * score_scale * jax.nn.sigmoid(-labels * (score_scale * scores + score_shift))
    pulled = jnp.dot(grad_scores, phrase_data, precision=lax.Precision.HIGHEST, preferred_element_type=jnp.float32)
    curve = lax.optimization_barrier(jnp.sum(grad_scores * scores, axis=1))
    grad_pooled = pulled / norms[:, None] - curve[:, None] * pooled / (D * norms[:, None] ** 2)
    grad_out = jnp.take(grad_pooled / counts[:, None], region_ids, axis=0).astype(jnp.bfloat16)
    pre_data = hidden_pre.astype(jnp.float32)
    activated = jax.nn.gelu(pre_data, approximate=False).astype(jnp.bfloat16)
    grad_w_out = lax.dot_general(activated, grad_out, (((0,), (0,)), ((), ())), preferred_element_type=jnp.float32).astype(jnp.bfloat16)
    grad_act = lax.dot_general(grad_out, w_out, (((1,), (1,)), ((), ())), preferred_element_type=jnp.float32)
    grad_hidden = (grad_act * gelu_slope(pre_data)).astype(jnp.bfloat16)
    grad_w_in = lax.dot_general(block_in, grad_hidden, (((0,), (0,)), ((), ())), preferred_element_type=jnp.float32).astype(jnp.bfloat16)
    branch = lax.dot_general(grad_hidden, w_in, (((1,), (1,)), ((), ())), preferred_element_type=jnp.float32)
    grad_in = (grad_out.astype(jnp.float32) + branch).astype(jnp.bfloat16)
    return (grad_in, grad_w_in, grad_w_out)
```

```python
import jax
import jax.numpy as jnp
from jax import lax
from jax.experimental import pallas as pl
from jax.experimental.pallas import tpu as pltpu
from jax.sharding import PartitionSpec as P

score_scale = 3.0
score_shift = -2.0
epsilon = 1e-06
half_root = 0.7071067811865476
density_norm = 0.3989422804014327

MESH = pl.DeviceIdType.MESH
f32 = jnp.float32
bf16 = jnp.bfloat16
BLK = 32
DL = 384
FL = 768
FH = 384


def nt(a, b):
    return lax.dot_general(a, b, (((1,), (1,)), ((), ())), preferred_element_type=f32)


def nn(a, b):
    return lax.dot_general(a, b, (((1,), (0,)), ((), ())), preferred_element_type=f32)


def split3(v):
    hi = v.astype(bf16)
    rest = v - hi.astype(f32)
    mid = rest.astype(bf16)
    low = (rest - mid.astype(f32)).astype(bf16)
    return jnp.concatenate([hi, mid, low], axis=0)


def kernel(
    ids, pos, bi_own, bo_own, ph, h_any, win_any, wout_any,
    gi_out, go_out, gh_out, bi_out,
    ext, part, corebuf, xs, xr, tot, ag,
    go, bi, win, wout, hc, slope, pact, pown, pcore, pxs, pxr, ysend, yrecv, gh, pbr, rbuf,
    lsem, osem, halo_s, halo_r, cs, cr, h7s, h7r, a7s, a7r,
    bis, bir, gos, gor, pcs, pcr, pxss, pxsr, yss, ysr, gxs, gxr, gcs, gcr, rs, rr,
):
    r = lax.axis_index("row")
    c = lax.axis_index("col")
    x, yh, k = r // 4, (r // 2) % 2, r % 2
    z, yl = c // 4, c % 4
    ko = 1 - k

    def rdev(xx, yy, kk):
        return (xx * 4 + yy * 2 + kk, c)

    def cdev(cc):
        return (r, cc)

    def rcopy(src, dst, ssem, rsem, dev):
        return pltpu.make_async_remote_copy(
            src_ref=src, dst_ref=dst, send_sem=ssem, recv_sem=rsem,
            device_id=dev, device_id_type=MESH,
        )

    loads = [
        pltpu.make_async_copy(wout_any, wout, lsem.at[0]),
        pltpu.make_async_copy(win_any, win, lsem.at[1]),
        pltpu.make_async_copy(
            h_any.at[:, x, :, pl.ds(pl.multiple_of(k * FH, 128), FH)], hc, lsem.at[2]
        ),
    ]
    for cp in loads:
        cp.start()

    barrier = pltpu.get_barrier_semaphore()
    peers7 = [(dx, dy) for dx in range(4) for dy in range(2) if (dx, dy) != (0, 0)]
    rows = [rdev((x + dx) % 4, (yh + dy) % 2, k) for dx, dy in peers7]
    rows += [rdev((x + dx) % 4, yh, ko) for dx in range(4)]
    for dev in rows:
        pl.semaphore_signal(barrier, inc=1, device_id=dev, device_id_type=MESH)

    def greet(d, _):
        pl.semaphore_signal(
            barrier, inc=1, device_id=cdev((c + d) % 32), device_id_type=MESH
        )
        return 0

    lax.fori_loop(1, 32, greet, 0)
    pl.semaphore_wait(barrier, len(rows) + 31)

    right = rcopy(bo_own, ext.at[pl.ds(0, BLK)], halo_s.at[0], halo_r.at[0], cdev((c + 1) % 32))
    left = rcopy(bo_own, ext.at[pl.ds(2 * BLK, BLK)], halo_s.at[1], halo_r.at[1], cdev((c + 31) % 32))
    right.start()
    left.start()
    ext[pl.ds(BLK, BLK), :] = bo_own[...]
    ext[pl.ds(3 * BLK, BLK), :] = jnp.zeros((BLK, DL), bf16)

    lane = lax.broadcasted_iota(jnp.int32, (BLK, 128), 1)
    sub = lax.broadcasted_iota(jnp.int32, (BLK, 128), 0)

    def ids_column(b):
        line = ids[pl.ds(b // 4, 1), :].astype(f32)
        return jnp.sum(jnp.where(lane == (b % 4) * BLK + sub, line, 0.0), axis=1, keepdims=True)

    own_col = ids_column(c)
    line = jnp.where(lane[:1] >= 3 * BLK, -1.0, 0.0)
    for n, b in enumerate(((c + 31) % 32, c, (c + 1) % 32)):
        col = own_col if n == 1 else ids_column(b)
        line += jnp.sum(jnp.where(lane == n * BLK + sub, col, 0.0), axis=0, keepdims=True)
    member = jnp.where(own_col == line, 1.0, 0.0).astype(f32)
    counts = jnp.sum(member, axis=1, keepdims=True)
    pos_col = jnp.zeros((BLK, 1), f32)
    for j in range(4):
        hit = own_col == (lane + j * 128).astype(f32)
        pos_col += jnp.sum(jnp.where(hit, pos[j : j + 1, :].astype(f32), 0.0), axis=1, keepdims=True)

    right.wait()
    left.wait()
    pooled = nn(member.astype(bf16), ext[...]) / counts
    inner3 = nt(split3(pooled), ph[...])
    inner = inner3[:BLK] + (inner3[BLK : 2 * BLK] + inner3[2 * BLK :])
    squares = jnp.sum(pooled * pooled, axis=1, keepdims=True)
    for j in range(4):
        part[j] = inner[:, j * 128 : (j + 1) * 128]
    part[4] = jnp.broadcast_to(squares, (BLK, 128))

    mine = pl.ds(pl.multiple_of(k * 16, 16), 16)
    theirs = pl.ds(pl.multiple_of(ko * 16, 16), 16)
    cp = rcopy(part.at[:, theirs, :], corebuf, cs, cr, rdev(x, yh, ko))
    cp.start()
    cp.wait()
    for j in range(4):
        xs[j, 0] = part[j, mine, :] + corebuf[j]
        xs[j, 1] = part[4, mine, :] + corebuf[4]
    sends = []
    for i, (dx, dy) in enumerate(peers7):
        xx = (x + dx) % 4
        sends.append(rcopy(xs.at[xx], xr.at[i], h7s.at[i], h7r.at[i], rdev(xx, (yh + dy) % 2, k)))
    for cp in sends:
        cp.start()

    bi[c] = bi_own[...]

    def offset(i):
        half = (i + 1) // 2
        return (i % 2) * half + (1 - i % 2) * (32 - half)

    def bi_send(i, _):
        d = offset(i)
        rcopy(bi.at[c], bi.at[c], bis.at[d], bir.at[d], cdev((c + d) % 32)).start()
        return 0

    lax.fori_loop(1, 32, bi_send, 0)

    for cp in sends:
        cp.wait()
    total = xs[x]
    for i in range(7):
        total += xr[i]
    tot[...] = total
    ag[k, x] = total
    sends = []
    for i, (dx, dk) in enumerate(peers7):
        sends.append(
            rcopy(tot, ag.at[k, x], a7s.at[i], a7r.at[i], rdev((x + dx) % 4, yh, (k + dk) % 2))
        )
    for cp in sends:
        cp.start()
    for cp in sends:
        cp.wait()

    inner = jnp.concatenate(
        [jnp.concatenate([ag[kk, j, 0] for j in range(4)], axis=1) for kk in range(2)], axis=0
    )
    squares = jnp.concatenate([ag[kk, 0, 1] for kk in range(2)], axis=0)[:, :1]
    width = float(16 * DL)
    norms = jnp.sqrt(squares / width + epsilon)
    scores = inner / norms
    phrase = lax.broadcasted_iota(jnp.int32, (BLK, 512), 1).astype(f32)
    labels = jnp.where(phrase == pos_col, 1.0, -1.0).astype(f32)
    grads = -labels * score_scale * jax.nn.sigmoid(-labels * (score_scale * scores + score_shift))
    pulled3 = nn(split3(grads), ph[...])
    pulled = pulled3[:BLK] + (pulled3[BLK : 2 * BLK] + pulled3[2 * BLK :])
    curve = jnp.sum(grads * scores, axis=1, keepdims=True)
    grad_pooled = pulled / norms - curve * pooled / (width * norms * norms)
    go[yl, z] = (grad_pooled / counts).astype(bf16)

    def go_send(i, _):
        d = offset(i)
        rcopy(go.at[yl, z], go.at[yl, z], gos.at[d], gor.at[d], cdev((c + d) % 32)).start()
        return 0

    lax.fori_loop(1, 32, go_send, 0)

    for cp in loads:
        cp.wait()

    def slope_step(i, _):
        v = hc[i].astype(f32)
        slope[i] = 0.5 * (1.0 + lax.erf(v * half_root)) + v * jnp.exp(-0.5 * v * v) * density_norm
        return 0

    lax.fori_loop(0, 8, slope_step, 0)

    def go_wait(i, _):
        d = offset(i)
        src = (c + 32 - d) % 32
        slot = go.at[src % 4, src // 4]
        rcopy(slot, slot, gos.at[d], gor.at[d], cdev((c + d) % 32)).wait_recv()
        return 0

    lax.fori_loop(1, 32, go_wait, 0)
    go_outs = [pltpu.make_async_copy(go.at[q], go_out.at[:, q], osem.at[q]) for q in range(4)]
    for cp in go_outs:
        cp.start()

    def other_half(i, _):
        q = (x + 1 + i) % 4
        w = wout[pl.ds(pl.multiple_of(ko * FH, 128), FH), :]
        pact[q] = nt(go[q].reshape(8 * BLK, DL), w).astype(bf16)
        rcopy(pact.at[q], pcore.at[q], pcs.at[q], pcr.at[q], rdev(x, yh, ko)).start()
        return 0

    lax.fori_loop(0, 4, other_half, 0)

    def own_half(i, _):
        q = (x + 1 + i) % 4
        w = wout[pl.ds(pl.multiple_of(k * FH, 128), FH), :]
        pown[q] = nt(go[q].reshape(8 * BLK, DL), w)
        return 0

    lax.fori_loop(0, 4, own_half, 0)

    for i in range(3):
        q = (x + 1 + i) % 4
        rcopy(pact.at[q], pcore.at[q], pcs.at[q], pcr.at[q], rdev(x, yh, ko)).wait()
        pxs[i] = (pown[q] + pcore[q].astype(f32)).astype(bf16)
        rcopy(pxs.at[i], pxr.at[i], pxss.at[i], pxsr.at[i], rdev(q, yh, k)).start()
    rcopy(pact.at[x], pcore.at[x], pcs.at[x], pcr.at[x], rdev(x, yh, ko)).wait()
    acc = pown[x] + pcore[x].astype(f32)
    for i in range(3):
        q = (x + 1 + i) % 4
        rcopy(pxs.at[i], pxr.at[i], pxss.at[i], pxsr.at[i], rdev(q, yh, k)).wait()
        acc += pxr[i].astype(f32)
    pown[x] = acc
    ysend[...] = acc.astype(bf16)
    cp = rcopy(ysend, yrecv, yss, ysr, rdev(x, 1 - yh, k))
    cp.start()
    cp.wait()
    full = pown[x] + yrecv[...].astype(f32)
    gh[k, x] = (full * slope[...].reshape(8 * BLK, FH)).astype(bf16)

    xsends = []
    for i in range(3):
        xsends.append(
            rcopy(gh.at[k, x], gh.at[k, x], gxs.at[i], gxr.at[i], rdev((x + 1 + i) % 4, yh, k))
        )
    for cp in xsends:
        cp.start()

    def core_send(q):
        return rcopy(gh.at[k, q], gh.at[k, q], gcs.at[q], gcr.at[q], rdev(x, yh, ko))

    def core_recv(q):
        return rcopy(gh.at[ko, q], gh.at[ko, q], gcs.at[q], gcr.at[q], rdev(x, yh, ko))

    core_send(x).start()

    def branch(q):
        core_recv(q).wait_recv()
        val = nt(gh[0, q], win[:, :FH]) + nt(gh[1, q], win[:, FH:])
        pbr[q] = val.astype(bf16).reshape(8, BLK, DL)

        def scatter(j, _):
            zt = (z + j) % 8
            dst = zt * 4 + q
            d = (dst + 32 - c) % 32

            @pl.when(d != 0)
            def _():
                rcopy(pbr.at[q, zt], rbuf.at[d], rs.at[d], rr.at[d], cdev(dst)).start()

            return 0

        lax.fori_loop(0, 8, scatter, 0)

    branch(x)
    for i in range(3):
        q = (x + 3 - i) % 4
        rcopy(gh.at[k, q], gh.at[k, q], gxs.at[i], gxr.at[i], rdev((x + 1 + i) % 4, yh, k)).wait_recv()
        core_send(q).start()
        branch(q)

    gh_outs = [
        pltpu.make_async_copy(
            gh.at[kk, q], gh_out.at[kk, q], osem.at[4 + kk * 4 + q]
        )
        for kk in range(2)
        for q in range(4)
    ]
    for cp in gh_outs:
        cp.start()

    def bi_wait(i, _):
        d = offset(i)
        src = (c + 32 - d) % 32
        rcopy(bi.at[src], bi.at[src], bis.at[d], bir.at[d], cdev((c + d) % 32)).wait_recv()
        return 0

    lax.fori_loop(1, 32, bi_wait, 0)
    bi_cp = pltpu.make_async_copy(bi, bi_out, osem.at[12])
    bi_cp.start()

    pown[0, pl.ds(0, BLK), :] = go[yl, z].astype(f32) + pbr[yl, z].astype(f32)

    def collect(d, _):
        rcopy(rbuf.at[d], rbuf.at[d], rs.at[d], rr.at[d], cdev((c + d) % 32)).wait_recv()
        pown[0, pl.ds(0, BLK), :] = pown[0, pl.ds(0, BLK), :] + rbuf[d].astype(f32)
        return 0

    lax.fori_loop(1, 32, collect, 0)
    gi_out[...] = pown[0, pl.ds(0, BLK), :].astype(bf16)

    for cp in xsends:
        cp.wait_send()
    for q in range(4):
        core_send(q).wait_send()

    def drain(d, _):
        rcopy(bi.at[c], bi.at[c], bis.at[d], bir.at[d], cdev((c + d) % 32)).wait_send()
        rcopy(go.at[yl, z], go.at[yl, z], gos.at[d], gor.at[d], cdev((c + d) % 32)).wait_send()
        rcopy(pbr.at[0, 0], rbuf.at[d], rs.at[d], rr.at[d], cdev((c + d) % 32)).wait_send()
        return 0

    lax.fori_loop(1, 32, drain, 0)
    for cp in go_outs + gh_outs + [bi_cp]:
        cp.wait()


def local(block_in, block_out, hidden_pre, w_in, w_out, phrases, region_ids, positive_phrase):
    dma = pltpu.SemaphoreType.DMA
    vm = pltpu.VMEM
    vspec = pl.BlockSpec(memory_space=pltpu.VMEM)
    aspec = pl.BlockSpec(memory_space=pl.ANY)
    gi, go, gh, bi = pl.pallas_call(
        kernel,
        out_shape=(
            jax.ShapeDtypeStruct((BLK, DL), bf16),
            jax.ShapeDtypeStruct((8, 4, BLK, DL), bf16),
            jax.ShapeDtypeStruct((2, 4, 8 * BLK, FH), bf16),
            jax.ShapeDtypeStruct((32, BLK, DL), bf16),
        ),
        in_specs=[vspec] * 5 + [aspec] * 3,
        out_specs=(vspec, aspec, aspec, aspec),
        scratch_shapes=[
            vm((4 * BLK, DL), bf16),
            vm((5, BLK, 128), f32),
            vm((5, 16, 128), f32),
            vm((4, 2, 16, 128), f32),
            vm((7, 2, 16, 128), f32),
            vm((2, 16, 128), f32),
            vm((2, 4, 2, 16, 128), f32),
            vm((4, 8, BLK, DL), bf16),
            vm((32, BLK, DL), bf16),
            vm((DL, FL), bf16),
            vm((FL, DL), bf16),
            vm((8, BLK, FH), bf16),
            vm((8, BLK, FH), f32),
            vm((4, 8 * BLK, FH), bf16),
            vm((4, 8 * BLK, FH), f32),
            vm((4, 8 * BLK, FH), bf16),
            vm((3, 8 * BLK, FH), bf16),
            vm((3, 8 * BLK, FH), bf16),
            vm((8 * BLK, FH), bf16),
            vm((8 * BLK, FH), bf16),
            vm((2, 4, 8 * BLK, FH), bf16),
            vm((4, 8, BLK, DL), bf16),
            vm((32, BLK, DL), bf16),
            dma((3,)), dma((13,)), dma((2,)), dma((2,)), dma, dma, dma((7,)), dma((7,)), dma((7,)), dma((7,)),
            dma((32,)), dma((32,)), dma((32,)), dma((32,)), dma((4,)), dma((4,)), dma((3,)), dma((3,)), dma, dma,
            dma((3,)), dma((3,)), dma((4,)), dma((4,)), dma((32,)), dma((32,)),
        ],
        compiler_params=pltpu.CompilerParams(
            collective_id=0, has_side_effects=True, vmem_limit_bytes=40 * 2**20
        ),
        name="mlp_backward",
    )(
        region_ids.reshape(8, 128),
        positive_phrase.reshape(4, 128),
        block_in,
        block_out,
        phrases,
        hidden_pre.reshape(8, 4, BLK, FL),
        w_in,
        w_out,
    )
    go = go.reshape(1024, DL)
    gh = gh.reshape(2, 4, 8, BLK, FH).transpose(2, 1, 3, 0, 4).reshape(1024, FL)
    bi = bi.reshape(1024, DL)
    act = jax.nn.gelu(hidden_pre.astype(f32), approximate=False).astype(bf16)
    tn = (((0,), (0,)), ((), ()))
    grad_w_out = lax.dot_general(act, go, tn, preferred_element_type=f32).astype(bf16)
    grad_w_in = lax.dot_general(bi, gh, tn, preferred_element_type=f32).astype(bf16)
    return gi, grad_w_in, grad_w_out


def solution(mesh):
    in_specs = (
        P("col", "row"),
        P("col", "row"),
        P(None, "col"),
        P("row", "col"),
        P("col", "row"),
        P(None, "row"),
        P(),
        P(),
    )
    out_specs = (P("col", "row"), P("row", "col"), P("col", "row"))
    return jax.shard_map(local, mesh=mesh, in_specs=in_specs, out_specs=out_specs, check_vma=False)
```

```python
import jax
import jax.numpy as jnp
from jax import lax
from jax.experimental import pallas as pl
from jax.experimental.pallas import tpu as pltpu
from jax.sharding import PartitionSpec as P

score_scale = 3.0
score_shift = -2.0
epsilon = 1e-06
half_root = 0.7071067811865476
density_norm = 0.3989422804014327

MESH = pl.DeviceIdType.MESH
f32 = jnp.float32
bf16 = jnp.bfloat16
BLK = 32
DL = 384
FL = 768
FH = 384


GROUPS = 4


def away(place):
    return (place % 2) * ((place + 1) // 2) + (1 - place % 2) * (8 - place // 2)


def nt(a, b):
    return lax.dot_general(a, b, (((1,), (1,)), ((), ())), preferred_element_type=f32)


def nn(a, b):
    return lax.dot_general(a, b, (((1,), (0,)), ((), ())), preferred_element_type=f32)


def tn(a, b):
    return lax.dot_general(a, b, (((0,), (0,)), ((), ())), preferred_element_type=f32)


def split3(v):
    hi = v.astype(bf16)
    rest = v - hi.astype(f32)
    mid = rest.astype(bf16)
    low = (rest - mid.astype(f32)).astype(bf16)
    return jnp.concatenate([hi, mid, low], axis=0)


def kernel(
    ids, pos, bi_own, bo_hbm, ph_hbm, h_hbm, win_hbm, wout_hbm,
    gi_out, dwin_out, dwout_out,
    bo_own, ph, ext, part, corebuf, xs, xr, tot, ag,
    go, bi, win, wout, hv, act, slope, dwout, dwin, dwout_b, dwin_b, pact, pown, pcore, acc, pxs, pxr, ysend, yrecv, gh, pbr, rbuf, gsum,
    lsem, osem, halo_s, halo_r, cs, cr, h7s, h7r, a7s, a7r,
    bis, bir, gos, gor, pcs, pcr, pxss, pxsr, yss, ysr, gxs, gxr, gcs, gcr, rs, rr,
):
    r = lax.axis_index("row")
    c = lax.axis_index("col")
    x, yh, k = r // 4, (r // 2) % 2, r % 2
    z, yl = c // 4, c % 4
    ko = 1 - k

    def rdev(xx, yy, kk):
        return (xx * 4 + yy * 2 + kk, c)

    def cdev(cc):
        return (r, cc)

    def rcopy(src, dst, ssem, rsem, dev):
        return pltpu.make_async_remote_copy(
            src_ref=src, dst_ref=dst, send_sem=ssem, recv_sem=rsem,
            device_id=dev, device_id_type=MESH,
        )

    loads = [
        pltpu.make_async_copy(src, dst, lsem.at[n])
        for n, (src, dst) in enumerate(
            ((bo_hbm, bo_own), (bi_own, bi.at[0, yl, 0]), (ph_hbm, ph), (wout_hbm, wout), (win_hbm, win))
        )
    ]
    loads += [
        pltpu.make_async_copy(
            h_hbm.at[(z + away(p)) % 8], hv.at[p // 2, :, p % 2], lsem.at[5 + p]
        )
        for p in range(8)
    ]
    for cp in loads:
        cp.start()

    barrier = pltpu.get_barrier_semaphore()
    peers7 = [(dx, dy) for dx in range(4) for dy in range(2) if (dx, dy) != (0, 0)]
    rows = [rdev((x + dx) % 4, (yh + dy) % 2, k) for dx, dy in peers7]
    rows += [rdev((x + dx) % 4, yh, ko) for dx in range(4)]
    for dev in rows:
        pl.semaphore_signal(barrier, inc=1, device_id=dev, device_id_type=MESH)

    def greet(d, _):
        pl.semaphore_signal(
            barrier, inc=1, device_id=cdev((c + d) % 32), device_id_type=MESH
        )
        return 0

    lax.fori_loop(1, 32, greet, 0)
    pl.semaphore_wait(barrier, len(rows) + 31)

    for cp in loads[:2]:
        cp.wait()

    right = rcopy(bo_own, ext.at[pl.ds(0, BLK)], halo_s.at[0], halo_r.at[0], cdev((c + 1) % 32))
    left = rcopy(bo_own, ext.at[pl.ds(2 * BLK, BLK)], halo_s.at[1], halo_r.at[1], cdev((c + 31) % 32))
    right.start()
    left.start()
    ext[pl.ds(BLK, BLK), :] = bo_own[...]
    ext[pl.ds(3 * BLK, BLK), :] = jnp.zeros((BLK, DL), bf16)

    def spread(buf, send, recv, n):
        place, to = n // 4, n % 4
        dev = cdev(((z + 8 - away(place)) % 8) * 4 + to)
        return rcopy(buf.at[0, yl, 0], buf.at[place // 2, yl, place % 2], send.at[n], recv.at[place * 4 + yl], dev)

    def landed(buf, send, recv, n):
        place, of = n // 4, n % 4
        slot = buf.at[place // 2, of, place % 2]
        return rcopy(slot, slot, send.at[n], recv.at[n], cdev(((z + away(place)) % 8) * 4 + of))

    def each(lo, hi, step):
        def body(n, _):
            @pl.when(n != yl)
            def _():
                step(n)

            return 0

        lax.fori_loop(4 * lo, 4 * hi, body, 0)

    each(0, 8, lambda n: spread(bi, bis, bir, n).start())

    lane = lax.broadcasted_iota(jnp.int32, (BLK, 128), 1)
    sub = lax.broadcasted_iota(jnp.int32, (BLK, 128), 0)

    def ids_column(b):
        line = ids[pl.ds(b // 4, 1), :].astype(f32)
        return jnp.sum(jnp.where(lane == (b % 4) * BLK + sub, line, 0.0), axis=1, keepdims=True)

    own_col = ids_column(c)
    line = jnp.where(lane[:1] >= 3 * BLK, -1.0, 0.0)
    for n, b in enumerate(((c + 31) % 32, c, (c + 1) % 32)):
        col = own_col if n == 1 else ids_column(b)
        line += jnp.sum(jnp.where(lane == n * BLK + sub, col, 0.0), axis=0, keepdims=True)
    member = jnp.where(own_col == line, 1.0, 0.0).astype(f32)
    counts = jnp.sum(member, axis=1, keepdims=True)
    pos_col = jnp.zeros((BLK, 1), f32)
    for j in range(4):
        hit = own_col == (lane + j * 128).astype(f32)
        pos_col += jnp.sum(jnp.where(hit, pos[j : j + 1, :].astype(f32), 0.0), axis=1, keepdims=True)

    loads[2].wait()
    right.wait()
    left.wait()
    pooled = nn(member.astype(bf16), ext[...]) / counts
    inner3 = nt(split3(pooled), ph[...])
    inner = inner3[:BLK] + (inner3[BLK : 2 * BLK] + inner3[2 * BLK :])
    squares = jnp.sum(pooled * pooled, axis=1, keepdims=True)
    for j in range(4):
        part[j] = inner[:, j * 128 : (j + 1) * 128]
    part[4] = jnp.broadcast_to(squares, (BLK, 128))

    mine = pl.ds(pl.multiple_of(k * 16, 16), 16)
    theirs = pl.ds(pl.multiple_of(ko * 16, 16), 16)
    cp = rcopy(part.at[:, theirs, :], corebuf, cs, cr, rdev(x, yh, ko))
    cp.start()
    cp.wait()
    for j in range(4):
        xs[j, 0] = part[j, mine, :] + corebuf[j]
        xs[j, 1] = part[4, mine, :] + corebuf[4]
    sends = []
    for i, (dx, dy) in enumerate(peers7):
        xx = (x + dx) % 4
        sends.append(rcopy(xs.at[xx], xr.at[i], h7s.at[i], h7r.at[i], rdev(xx, (yh + dy) % 2, k)))
    for cp in sends:
        cp.start()


    for cp in loads[5:]:
        cp.wait()

    def act_step(n, _):
        g, q, i = n // 8, (n // 2) % 4, n % 2
        v = hv[g, q, i].astype(f32)
        act[g, q, i] = (0.5 * v * (1.0 + lax.erf(v * half_root))).astype(bf16)
        return 0

    lax.fori_loop(0, 16, act_step, 0)

    for cp in sends:
        cp.wait()
    total = xs[x]
    for i in range(7):
        total += xr[i]
    tot[...] = total
    ag[k, x] = total
    sends = []
    for i, (dx, dk) in enumerate(peers7):
        sends.append(
            rcopy(tot, ag.at[k, x], a7s.at[i], a7r.at[i], rdev((x + dx) % 4, yh, (k + dk) % 2))
        )
    for cp in sends:
        cp.start()

    lax.fori_loop(16, 32, act_step, 0)

    def slope_step(n, _):
        v = hv[n // 2, x, n % 2, :, pl.ds(pl.multiple_of(k * FH, 128), FH)].astype(f32)
        slope[n] = 0.5 * (1.0 + lax.erf(v * half_root)) + v * jnp.exp(-0.5 * v * v) * density_norm
        return 0

    lax.fori_loop(0, 8, slope_step, 0)

    for cp in sends:
        cp.wait()

    inner = jnp.concatenate(
        [jnp.concatenate([ag[kk, j, 0] for j in range(4)], axis=1) for kk in range(2)], axis=0
    )
    squares = jnp.concatenate([ag[kk, 0, 1] for kk in range(2)], axis=0)[:, :1]
    width = float(16 * DL)
    norms = jnp.sqrt(squares / width + epsilon)
    scores = inner / norms
    phrase = lax.broadcasted_iota(jnp.int32, (BLK, 512), 1).astype(f32)
    labels = jnp.where(phrase == pos_col, 1.0, -1.0).astype(f32)
    grads = -labels * score_scale * jax.nn.sigmoid(-labels * (score_scale * scores + score_shift))
    pulled3 = nn(split3(grads), ph[...])
    pulled = pulled3[:BLK] + (pulled3[BLK : 2 * BLK] + pulled3[2 * BLK :])
    curve = jnp.sum(grads * scores, axis=1, keepdims=True)
    grad_pooled = pulled / norms - curve * pooled / (width * norms * norms)
    go[0, yl, 0] = (grad_pooled / counts).astype(bf16)

    each(0, 8, lambda n: spread(go, gos, gor, n).start())

    for cp in loads[3:5]:
        cp.wait()

    whalf = [wout.at[pl.ds(pl.multiple_of(kk * FH, 128), FH), :] for kk in (ko, k)]

    def core_sum(g):
        return rcopy(pact.at[g], pcore.at[g], pcs.at[g], pcr.at[g], rdev(x, yh, ko))

    def x_sum(g, i):
        n = g * 3 + i
        return rcopy(pxs.at[n], pxr.at[n], pxss.at[n], pxsr.at[n], rdev((x + 1 + i) % 4, yh, k))

    def y_sum(g):
        return rcopy(ysend.at[g], yrecv.at[g], yss.at[g], ysr.at[g], rdev(x, 1 - yh, k))

    def x_back(g, i):
        slot = gh.at[k, g, x]
        return rcopy(slot, slot, gxs.at[g * 3 + i], gxr.at[g * 3 + i], rdev((x + 1 + i) % 4, yh, k))

    def x_backed(g, i):
        slot = gh.at[k, g, (x + 3 - i) % 4]
        return rcopy(slot, slot, gxs.at[g * 3 + i], gxr.at[g * 3 + i], rdev((x + 1 + i) % 4, yh, k))

    def core_back(g, q, kk):
        slot = gh.at[kk, g, q]
        return rcopy(slot, slot, gcs.at[g * 4 + q], gcr.at[g * 4 + q], rdev(x, yh, ko))

    def term(n):
        place, to = n // 4, n % 4
        dev = cdev(((z + away(place)) % 8) * 4 + to)
        return rcopy(pbr.at[place // 2, to, place % 2], rbuf.at[place * 4 + yl], rs.at[n], rr.at[place * 4 + yl], dev)

    def product(g):
        each(2 * g, 2 * g + 2, lambda n: landed(go, gos, gor, n).wait_recv())
        a = go[g].reshape(8 * BLK, DL)
        pact[g] = nt(a, whalf[0][...]).astype(bf16).reshape(4, 2, BLK, FH)
        core_sum(g).start()
        pown[g] = nt(a, whalf[1][...]).reshape(4, 2, BLK, FH)

    def to_x(g):
        core_sum(g).wait()
        for i in range(3):
            q = (x + 1 + i) % 4
            pxs[g * 3 + i] = (pown[g, q] + pcore[g, q].astype(f32)).astype(bf16)
            x_sum(g, i).start()
        acc[g] = pown[g, x] + pcore[g, x].astype(f32)

    def to_y(g):
        for i in range(3):
            x_sum(g, i).wait()
        val = acc[g]
        for i in range(3):
            val += pxr[g * 3 + i].astype(f32)
        acc[g] = val
        ysend[g] = val.astype(bf16)
        y_sum(g).start()

    def hidden(g):
        y_sum(g).wait()
        full = acc[g] + yrecv[g].astype(f32)
        gh[k, g, x] = (full * slope[2 * g : 2 * g + 2]).astype(bf16)
        for i in range(3):
            x_back(g, i).start()
        core_back(g, x, k).start()

    def forward(g):
        for i in range(3):
            x_backed(g, i).wait_recv()
            core_back(g, (x + 3 - i) % 4, k).start()

    def branch(g):
        for q in range(4):
            core_back(g, q, ko).wait_recv()
        val = nt(gh[0, g].reshape(8 * BLK, FH), win[:, :FH]) + nt(gh[1, g].reshape(8 * BLK, FH), win[:, FH:])
        pbr[g] = val.astype(bf16).reshape(4, 2, BLK, DL)
        each(2 * g, 2 * g + 2, lambda n: term(n).start())

    def weight_out(g):
        val = tn(act[g].reshape(8 * BLK, FL), go[g].reshape(8 * BLK, DL))
        if g:
            val += dwout[...]
        if g < GROUPS - 1:
            dwout[...] = val
        else:
            dwout_b[...] = val.astype(bf16)
            dwout_cp.start()

    def weight_in(g):
        for kk in range(2):
            val = tn(bi[g].reshape(8 * BLK, DL), gh[kk, g].reshape(8 * BLK, FH))
            if g:
                val += dwin[kk]
            if g < GROUPS - 1:
                dwin[kk] = val
            else:
                dwin_b[:, kk * FH : (kk + 1) * FH] = val.astype(bf16)
        if g == GROUPS - 1:
            dwin_cp.start()

    dwout_cp = pltpu.make_async_copy(dwout_b, dwout_out, osem.at[0])
    dwin_cp = pltpu.make_async_copy(dwin_b, dwin_out, osem.at[1])

    steps = (branch, forward, hidden, to_y, to_x, product)
    for t in range(GROUPS + len(steps) - 1):
        for late, step in enumerate(steps):
            g = t - (len(steps) - 1 - late)
            if 0 <= g < GROUPS:
                step(g)
        if 0 <= t - 1 < GROUPS:
            weight_out(t - 1)
        if t == GROUPS:
            each(0, 8, lambda n: landed(bi, bis, bir, n).wait_recv())
        if 0 <= t - 5 < GROUPS:
            weight_in(t - 5)

    gsum[...] = go[0, yl, 0].astype(f32) + pbr[0, yl, 0].astype(f32)

    def collect(n):
        slot = rbuf.at[n]
        rcopy(slot, slot, rs.at[n], rr.at[n], cdev((c + 1) % 32)).wait_recv()
        gsum[...] += rbuf[n].astype(f32)

    each(0, 8, collect)
    gi_out[...] = gsum[...].astype(bf16)

    for g in range(GROUPS):
        for i in range(3):
            x_back(g, i).wait_send()
        for q in range(4):
            core_back(g, q, k).wait_send()

    def drain(n):
        spread(bi, bis, bir, n).wait_send()
        spread(go, gos, gor, n).wait_send()
        term(n).wait_send()

    each(0, 8, drain)
    dwout_cp.wait()
    dwin_cp.wait()


def local(block_in, block_out, hidden_pre, w_in, w_out, phrases, region_ids, positive_phrase):
    dma = pltpu.SemaphoreType.DMA
    vm = pltpu.VMEM
    vspec = pl.BlockSpec(memory_space=pltpu.VMEM)
    hspec = pl.BlockSpec(memory_space=pltpu.HBM)
    gi, dwin, dwout = pl.pallas_call(
        kernel,
        out_shape=(
            jax.ShapeDtypeStruct((BLK, DL), bf16),
            jax.ShapeDtypeStruct((DL, FL), bf16),
            jax.ShapeDtypeStruct((FL, DL), bf16),
        ),
        in_specs=[vspec] * 2 + [hspec] * 6,
        out_specs=(vspec, hspec, hspec),
        scratch_shapes=[
            vm((BLK, DL), bf16),
            vm((512, DL), bf16),
            vm((4 * BLK, DL), bf16),
            vm((5, BLK, 128), f32),
            vm((5, 16, 128), f32),
            vm((4, 2, 16, 128), f32),
            vm((7, 2, 16, 128), f32),
            vm((2, 16, 128), f32),
            vm((2, 4, 2, 16, 128), f32),
            vm((4, 4, 2, BLK, DL), bf16),
            vm((4, 4, 2, BLK, DL), bf16),
            vm((DL, FL), bf16),
            vm((FL, DL), bf16),
            vm((4, 4, 2, BLK, FL), bf16),
            vm((4, 4, 2, BLK, FL), bf16),
            vm((8, BLK, FH), f32),
            vm((FL, DL), f32),
            vm((2, DL, FH), f32),
            vm((FL, DL), bf16),
            vm((DL, FL), bf16),
            vm((4, 4, 2, BLK, FH), bf16),
            vm((4, 4, 2, BLK, FH), f32),
            vm((4, 4, 2, BLK, FH), bf16),
            vm((4, 2, BLK, FH), f32),
            vm((12, 2, BLK, FH), bf16),
            vm((12, 2, BLK, FH), bf16),
            vm((4, 2, BLK, FH), bf16),
            vm((4, 2, BLK, FH), bf16),
            vm((2, 4, 4, 2, BLK, FH), bf16),
            vm((4, 4, 2, BLK, DL), bf16),
            vm((32, BLK, DL), bf16),
            vm((BLK, DL), f32),
            dma((13,)), dma((2,)), dma((2,)), dma((2,)), dma, dma, dma((7,)), dma((7,)), dma((7,)), dma((7,)),
            dma((32,)), dma((32,)), dma((32,)), dma((32,)), dma((4,)), dma((4,)), dma((12,)), dma((12,)), dma((4,)), dma((4,)),
            dma((12,)), dma((12,)), dma((16,)), dma((16,)), dma((32,)), dma((32,)),
        ],
        compiler_params=pltpu.CompilerParams(
            collective_id=0, has_side_effects=True, vmem_limit_bytes=60 * 2**20
        ),
        name="mlp_backward",
    )(
        region_ids.reshape(8, 128),
        positive_phrase.reshape(4, 128),
        block_in,
        block_out,
        phrases,
        hidden_pre.reshape(8, 4, BLK, FL),
        w_in,
        w_out,
    )
    return gi, dwin, dwout


def solution(mesh):
    in_specs = (
        P("col", "row"),
        P("col", "row"),
        P(None, "col"),
        P("row", "col"),
        P("col", "row"),
        P(None, "row"),
        P(),
        P(),
    )
    out_specs = (P("col", "row"), P("row", "col"), P("col", "row"))
    return jax.shard_map(local, mesh=mesh, in_specs=in_specs, out_specs=out_specs, check_vma=False)
```

```python
import jax
import jax.numpy as jnp
from jax import lax
from jax.experimental import pallas as pl
from jax.experimental.pallas import tpu as pltpu
from jax.sharding import PartitionSpec as P

score_scale = 3.0
score_shift = -2.0
epsilon = 1e-06
half_root = 0.7071067811865476
density_norm = 0.3989422804014327

MESH = pl.DeviceIdType.MESH
f32 = jnp.float32
bf16 = jnp.bfloat16
BLK = 32
DL = 384
FL = 768
FH = 384


GROUPS = 4
AWAY = (1, 7, 0, 4, 3, 5, 2, 6)
HOME = AWAY.index(0)
FAR = [AWAY.index(d) for d in (4, 3, 5)]
NEAR = [AWAY.index(d) for d in (1, 7, 2, 6)]


def at(buf, place, part):
    return buf.at[place // 2, part, place % 2]


def nt(a, b):
    return lax.dot_general(a, b, (((1,), (1,)), ((), ())), preferred_element_type=f32)


def nn(a, b):
    return lax.dot_general(a, b, (((1,), (0,)), ((), ())), preferred_element_type=f32)


def tn(a, b):
    return lax.dot_general(a, b, (((0,), (0,)), ((), ())), preferred_element_type=f32)


def split3(v):
    hi = v.astype(bf16)
    rest = v - hi.astype(f32)
    mid = rest.astype(bf16)
    low = (rest - mid.astype(f32)).astype(bf16)
    return jnp.concatenate([hi, mid, low], axis=0)


def kernel(
    ids, pos, bi_own, bo_hbm, ph_hbm, h_hbm, win_hbm, wout_hbm,
    gi_out, dwin_out, dwout_out,
    bo_own, ph, ext, part, corebuf, xs, xr, tot, ag,
    go, bi, win, wout, hv, act, slope, dwout, dwin, dwout_b, dwin_b, pact, pown, pcore, acc, pxs, pxr, ysend, yrecv, gh, pbr, rbuf, gsum,
    lsem, osem, halo_s, halo_r, cs, cr, h7s, h7r, a7s, a7r,
    bis, bir, brs, brr, gos, gor, fas, far, nes, ner, pcs, pcr, pxss, pxsr, yss, ysr, gxs, gxr, gcs, gcr, rs, rr,
):
    r = lax.axis_index("row")
    c = lax.axis_index("col")
    x, yh, k = r // 4, (r // 2) % 2, r % 2
    z, yl = c // 4, c % 4
    ko = 1 - k

    def rdev(xx, yy, kk):
        return (xx * 4 + yy * 2 + kk, c)

    def cdev(cc):
        return (r, cc)

    def rcopy(src, dst, ssem, rsem, dev):
        return pltpu.make_async_remote_copy(
            src_ref=src, dst_ref=dst, send_sem=ssem, recv_sem=rsem,
            device_id=dev, device_id_type=MESH,
        )

    loads = [
        pltpu.make_async_copy(src, dst, lsem.at[n])
        for n, (src, dst) in enumerate(
            ((bo_hbm, bo_own), (bi_own, at(bi, HOME, yl)), (ph_hbm, ph), (wout_hbm, wout), (win_hbm, win))
        )
    ]
    loads += [
        pltpu.make_async_copy(
            h_hbm.at[(z + AWAY[p]) % 8], hv.at[p // 2, :, p % 2], lsem.at[5 + p]
        )
        for p in range(8)
    ]
    for cp in loads:
        cp.start()

    barrier = pltpu.get_barrier_semaphore()
    peers7 = [(dx, dy) for dx in range(4) for dy in range(2) if (dx, dy) != (0, 0)]
    rows = [rdev((x + dx) % 4, (yh + dy) % 2, k) for dx, dy in peers7]
    rows += [rdev((x + dx) % 4, yh, ko) for dx in range(4)]
    for dev in rows:
        pl.semaphore_signal(barrier, inc=1, device_id=dev, device_id_type=MESH)

    def greet(d, _):
        pl.semaphore_signal(
            barrier, inc=1, device_id=cdev((c + d) % 32), device_id_type=MESH
        )
        return 0

    lax.fori_loop(1, 32, greet, 0)
    pl.semaphore_wait(barrier, len(rows) + 31)

    for cp in loads[:2]:
        cp.wait()

    right = rcopy(bo_own, ext.at[pl.ds(0, BLK)], halo_s.at[0], halo_r.at[0], cdev((c + 1) % 32))
    left = rcopy(bo_own, ext.at[pl.ds(2 * BLK, BLK)], halo_s.at[1], halo_r.at[1], cdev((c + 31) % 32))
    right.start()
    left.start()
    ext[pl.ds(BLK, BLK), :] = bo_own[...]
    ext[pl.ds(3 * BLK, BLK), :] = jnp.zeros((BLK, DL), bf16)

    def spread(buf, send, recv, place, to):
        n = place * 4 + to
        slot = at(buf, place, yl)
        return rcopy(slot, slot, send.at[n], recv.at[place * 4 + yl], cdev(z * 4 + to))

    def landed(buf, send, recv, place, of):
        n = place * 4 + of
        slot = at(buf, place, of)
        return rcopy(slot, slot, send.at[n], recv.at[n], cdev(z * 4 + of))

    def each(places, step, every=False):
        for place in places:

            def body(n, _):
                if every:
                    step(place, n)
                else:

                    @pl.when(n != yl)
                    def _():
                        step(place, n)

                return 0

            lax.fori_loop(0, 4, body, 0)

    def ring(step, back):
        src = AWAY.index(((step - 1) * (7 - 6 * back)) % 8)
        dst = AWAY.index((step * (7 - 6 * back)) % 8)
        half = pl.ds(0, 4) if step < 4 else pl.ds(2 * back, 2)
        n = 2 * step + back
        to = cdev(((z + 1 + 6 * back) % 8) * 4 + yl)
        return rcopy(at(bi, src, half), at(bi, dst, half), brs.at[n - 2], brr.at[n - 2], to)

    def ring_step(step):
        if step == 1:
            each((HOME,), lambda p, n: landed(bi, bis, bir, p, n).wait_recv())
        for back in range(2):
            if step > 1:
                ring(step - 1, back).wait_recv()
            if step < 5:
                ring(step, back).start()

    each((HOME,), lambda p, n: spread(bi, bis, bir, p, n).start())

    lane = lax.broadcasted_iota(jnp.int32, (BLK, 128), 1)
    sub = lax.broadcasted_iota(jnp.int32, (BLK, 128), 0)

    def ids_column(b):
        line = ids[pl.ds(b // 4, 1), :].astype(f32)
        return jnp.sum(jnp.where(lane == (b % 4) * BLK + sub, line, 0.0), axis=1, keepdims=True)

    own_col = ids_column(c)
    line = jnp.where(lane[:1] >= 3 * BLK, -1.0, 0.0)
    for n, b in enumerate(((c + 31) % 32, c, (c + 1) % 32)):
        col = own_col if n == 1 else ids_column(b)
        line += jnp.sum(jnp.where(lane == n * BLK + sub, col, 0.0), axis=0, keepdims=True)
    member = jnp.where(own_col == line, 1.0, 0.0).astype(f32)
    counts = jnp.sum(member, axis=1, keepdims=True)
    pos_col = jnp.zeros((BLK, 1), f32)
    for j in range(4):
        hit = own_col == (lane + j * 128).astype(f32)
        pos_col += jnp.sum(jnp.where(hit, pos[j : j + 1, :].astype(f32), 0.0), axis=1, keepdims=True)

    loads[2].wait()
    right.wait()
    left.wait()
    pooled = nn(member.astype(bf16), ext[...]) / counts
    inner3 = nt(split3(pooled), ph[...])
    inner = inner3[:BLK] + (inner3[BLK : 2 * BLK] + inner3[2 * BLK :])
    squares = jnp.sum(pooled * pooled, axis=1, keepdims=True)
    for j in range(4):
        part[j] = inner[:, j * 128 : (j + 1) * 128]
    part[4] = jnp.broadcast_to(squares, (BLK, 128))

    ring_step(1)

    mine = pl.ds(pl.multiple_of(k * 16, 16), 16)
    theirs = pl.ds(pl.multiple_of(ko * 16, 16), 16)
    cp = rcopy(part.at[:, theirs, :], corebuf, cs, cr, rdev(x, yh, ko))
    cp.start()
    cp.wait()
    for j in range(4):
        xs[j, 0] = part[j, mine, :] + corebuf[j]
        xs[j, 1] = part[4, mine, :] + corebuf[4]
    sends = []
    for i, (dx, dy) in enumerate(peers7):
        xx = (x + dx) % 4
        sends.append(rcopy(xs.at[xx], xr.at[i], h7s.at[i], h7r.at[i], rdev(xx, (yh + dy) % 2, k)))
    for cp in sends:
        cp.start()


    for cp in loads[5:]:
        cp.wait()

    def act_step(n, _):
        g, q, i = n // 8, (n // 2) % 4, n % 2
        v = hv[g, q, i].astype(f32)
        act[g, q, i] = (0.5 * v * (1.0 + lax.erf(v * half_root))).astype(bf16)
        return 0

    lax.fori_loop(0, 16, act_step, 0)
    ring_step(2)

    for cp in sends:
        cp.wait()
    total = xs[x]
    for i in range(7):
        total += xr[i]
    tot[...] = total
    ag[k, x] = total
    sends = []
    for i, (dx, dk) in enumerate(peers7):
        sends.append(
            rcopy(tot, ag.at[k, x], a7s.at[i], a7r.at[i], rdev((x + dx) % 4, yh, (k + dk) % 2))
        )
    for cp in sends:
        cp.start()

    lax.fori_loop(16, 32, act_step, 0)

    def slope_step(n, _):
        v = hv[n // 2, x, n % 2, :, pl.ds(pl.multiple_of(k * FH, 128), FH)].astype(f32)
        slope[n] = 0.5 * (1.0 + lax.erf(v * half_root)) + v * jnp.exp(-0.5 * v * v) * density_norm
        return 0

    lax.fori_loop(0, 8, slope_step, 0)
    ring_step(3)

    for cp in sends:
        cp.wait()

    inner = jnp.concatenate(
        [jnp.concatenate([ag[kk, j, 0] for j in range(4)], axis=1) for kk in range(2)], axis=0
    )
    squares = jnp.concatenate([ag[kk, 0, 1] for kk in range(2)], axis=0)[:, :1]
    width = float(16 * DL)
    norms = jnp.sqrt(squares / width + epsilon)
    scores = inner / norms
    phrase = lax.broadcasted_iota(jnp.int32, (BLK, 512), 1).astype(f32)
    labels = jnp.where(phrase == pos_col, 1.0, -1.0).astype(f32)
    grads = -labels * score_scale * jax.nn.sigmoid(-labels * (score_scale * scores + score_shift))
    pulled3 = nn(split3(grads), ph[...])
    pulled = pulled3[:BLK] + (pulled3[BLK : 2 * BLK] + pulled3[2 * BLK :])
    curve = jnp.sum(grads * scores, axis=1, keepdims=True)
    grad_pooled = pulled / norms - curve * pooled / (width * norms * norms)
    go[HOME // 2, yl, HOME % 2] = (grad_pooled / counts).astype(bf16)

    def to_far(n):
        place = FAR[n]
        dev = cdev(((z + 8 - AWAY[place]) % 8) * 4 + yl)
        return rcopy(at(go, HOME, yl), at(go, place, yl), fas.at[n], far.at[n], dev)

    def to_near(n):
        place = NEAR[n]
        dev = cdev(((z + 8 - AWAY[place]) % 8) * 4 + yl)
        return rcopy(at(go, HOME, pl.ds(0, 4)), at(go, place, pl.ds(0, 4)), nes.at[n], ner.at[n], dev)

    def go_landed(places):
        each(places, lambda p, n: landed(go, gos, gor, p, n).wait_recv())

    def go_spread(places):
        each(places, lambda p, n: spread(go, gos, gor, p, n).start())

    go_spread((HOME,))
    for n in range(3):
        to_far(n).start()
    go_landed((HOME,))
    for n in range(4):
        to_near(n).start()
    for n in range(3):
        to_far(n).wait_recv()
        go_spread(FAR[n : n + 1])

    for cp in loads[3:5]:
        cp.wait()

    whalf = [wout.at[pl.ds(pl.multiple_of(kk * FH, 128), FH), :] for kk in (ko, k)]

    def core_sum(g):
        return rcopy(pact.at[g], pcore.at[g], pcs.at[g], pcr.at[g], rdev(x, yh, ko))

    def x_sum(g, i):
        n = g * 3 + i
        return rcopy(pxs.at[n], pxr.at[n], pxss.at[n], pxsr.at[n], rdev((x + 1 + i) % 4, yh, k))

    def y_sum(g):
        return rcopy(ysend.at[g], yrecv.at[g], yss.at[g], ysr.at[g], rdev(x, 1 - yh, k))

    def x_back(g, i):
        slot = gh.at[k, g, x]
        return rcopy(slot, slot, gxs.at[g * 3 + i], gxr.at[g * 3 + i], rdev((x + 1 + i) % 4, yh, k))

    def x_backed(g, i):
        slot = gh.at[k, g, (x + 3 - i) % 4]
        return rcopy(slot, slot, gxs.at[g * 3 + i], gxr.at[g * 3 + i], rdev((x + 1 + i) % 4, yh, k))

    def core_back(g, q, kk):
        slot = gh.at[kk, g, q]
        return rcopy(slot, slot, gcs.at[g * 4 + q], gcr.at[g * 4 + q], rdev(x, yh, ko))

    def term(place, to):
        n = place * 4
        dev = cdev(((z + AWAY[place]) % 8) * 4 + to)
        return rcopy(at(pbr, place, to), rbuf.at[n + yl], rs.at[n + to], rr.at[n + yl], dev)

    def terms(places, step):
        for place in places:
            each((place,), step, every=place != HOME)

    def product(g):
        for place in (2 * g, 2 * g + 1):
            if place in NEAR:
                to_near(NEAR.index(place)).wait_recv()
            elif place in FAR:
                go_landed((place,))
        a = go[g].reshape(8 * BLK, DL)
        pact[g] = nt(a, whalf[0][...]).astype(bf16).reshape(4, 2, BLK, FH)
        core_sum(g).start()
        pown[g] = nt(a, whalf[1][...]).reshape(4, 2, BLK, FH)

    def to_x(g):
        core_sum(g).wait()
        for i in range(3):
            q = (x + 1 + i) % 4
            pxs[g * 3 + i] = (pown[g, q] + pcore[g, q].astype(f32)).astype(bf16)
            x_sum(g, i).start()
        acc[g] = pown[g, x] + pcore[g, x].astype(f32)

    def to_y(g):
        for i in range(3):
            x_sum(g, i).wait()
        val = acc[g]
        for i in range(3):
            val += pxr[g * 3 + i].astype(f32)
        acc[g] = val
        ysend[g] = val.astype(bf16)
        y_sum(g).start()

    def hidden(g):
        y_sum(g).wait()
        full = acc[g] + yrecv[g].astype(f32)
        gh[k, g, x] = (full * slope[2 * g : 2 * g + 2]).astype(bf16)
        for i in range(3):
            x_back(g, i).start()
        core_back(g, x, k).start()

    def forward(g):
        for i in range(3):
            x_backed(g, i).wait_recv()
            core_back(g, (x + 3 - i) % 4, k).start()

    def branch(g):
        for q in range(4):
            core_back(g, q, ko).wait_recv()
        val = nt(gh[0, g].reshape(8 * BLK, FH), win[:, :FH]) + nt(gh[1, g].reshape(8 * BLK, FH), win[:, FH:])
        pbr[g] = val.astype(bf16).reshape(4, 2, BLK, DL)
        terms((2 * g, 2 * g + 1), lambda p, n: term(p, n).start())

    def weight_out(g):
        val = tn(act[g].reshape(8 * BLK, FL), go[g].reshape(8 * BLK, DL))
        if g:
            val += dwout[...]
        if g < GROUPS - 1:
            dwout[...] = val
        else:
            dwout_b[...] = val.astype(bf16)
            dwout_cp.start()

    def weight_in(g):
        for kk in range(2):
            val = tn(bi[g].reshape(8 * BLK, DL), gh[kk, g].reshape(8 * BLK, FH))
            if g:
                val += dwin[kk]
            if g < GROUPS - 1:
                dwin[kk] = val
            else:
                dwin_b[:, kk * FH : (kk + 1) * FH] = val.astype(bf16)
        if g == GROUPS - 1:
            dwin_cp.start()

    dwout_cp = pltpu.make_async_copy(dwout_b, dwout_out, osem.at[0])
    dwin_cp = pltpu.make_async_copy(dwin_b, dwin_out, osem.at[1])

    steps = (branch, forward, hidden, to_y, to_x, product)
    for t in range(GROUPS + len(steps) - 1):
        for late, step in enumerate(steps):
            g = t - (len(steps) - 1 - late)
            if 0 <= g < GROUPS:
                step(g)
        if 0 <= t - 1 < GROUPS:
            weight_out(t - 1)
        if t == 1:
            ring_step(4)
        if t == GROUPS:
            ring_step(5)
        if 0 <= t - 5 < GROUPS:
            weight_in(t - 5)

    gsum[...] = go[HOME // 2, yl, HOME % 2].astype(f32) + pbr[HOME // 2, yl, HOME % 2].astype(f32)

    def collect(place, of):
        n = place * 4 + of
        slot = rbuf.at[n]
        rcopy(slot, slot, rs.at[n], rr.at[n], cdev((c + 1) % 32)).wait_recv()
        gsum[...] += rbuf[n].astype(f32)

    terms(range(8), collect)
    gi_out[...] = gsum[...].astype(bf16)

    for g in range(GROUPS):
        for i in range(3):
            x_back(g, i).wait_send()
        for q in range(4):
            core_back(g, q, k).wait_send()

    terms(range(8), lambda p, n: term(p, n).wait_send())
    each([HOME] + FAR, lambda p, n: spread(go, gos, gor, p, n).wait_send())
    for n in range(3):
        to_far(n).wait_send()
    for n in range(4):
        to_near(n).wait_send()
    each((HOME,), lambda p, n: spread(bi, bis, bir, p, n).wait_send())
    for step in range(1, 5):
        for back in range(2):
            ring(step, back).wait_send()
    dwout_cp.wait()
    dwin_cp.wait()


def local(block_in, block_out, hidden_pre, w_in, w_out, phrases, region_ids, positive_phrase):
    dma = pltpu.SemaphoreType.DMA
    vm = pltpu.VMEM
    vspec = pl.BlockSpec(memory_space=pltpu.VMEM)
    hspec = pl.BlockSpec(memory_space=pltpu.HBM)
    gi, dwin, dwout = pl.pallas_call(
        kernel,
        out_shape=(
            jax.ShapeDtypeStruct((BLK, DL), bf16),
            jax.ShapeDtypeStruct((DL, FL), bf16),
            jax.ShapeDtypeStruct((FL, DL), bf16),
        ),
        in_specs=[vspec] * 2 + [hspec] * 6,
        out_specs=(vspec, hspec, hspec),
        scratch_shapes=[
            vm((BLK, DL), bf16),
            vm((512, DL), bf16),
            vm((4 * BLK, DL), bf16),
            vm((5, BLK, 128), f32),
            vm((5, 16, 128), f32),
            vm((4, 2, 16, 128), f32),
            vm((7, 2, 16, 128), f32),
            vm((2, 16, 128), f32),
            vm((2, 4, 2, 16, 128), f32),
            vm((4, 4, 2, BLK, DL), bf16),
            vm((4, 4, 2, BLK, DL), bf16),
            vm((DL, FL), bf16),
            vm((FL, DL), bf16),
            vm((4, 4, 2, BLK, FL), bf16),
            vm((4, 4, 2, BLK, FL), bf16),
            vm((8, BLK, FH), f32),
            vm((FL, DL), f32),
            vm((2, DL, FH), f32),
            vm((FL, DL), bf16),
            vm((DL, FL), bf16),
            vm((4, 4, 2, BLK, FH), bf16),
            vm((4, 4, 2, BLK, FH), f32),
            vm((4, 4, 2, BLK, FH), bf16),
            vm((4, 2, BLK, FH), f32),
            vm((12, 2, BLK, FH), bf16),
            vm((12, 2, BLK, FH), bf16),
            vm((4, 2, BLK, FH), bf16),
            vm((4, 2, BLK, FH), bf16),
            vm((2, 4, 4, 2, BLK, FH), bf16),
            vm((4, 4, 2, BLK, DL), bf16),
            vm((32, BLK, DL), bf16),
            vm((BLK, DL), f32),
            dma((13,)), dma((2,)), dma((2,)), dma((2,)), dma, dma, dma((7,)), dma((7,)), dma((7,)), dma((7,)),
            dma((32,)), dma((32,)), dma((8,)), dma((8,)), dma((32,)), dma((32,)), dma((3,)), dma((3,)), dma((4,)), dma((4,)),
            dma((4,)), dma((4,)), dma((12,)), dma((12,)), dma((4,)), dma((4,)),
            dma((12,)), dma((12,)), dma((16,)), dma((16,)), dma((32,)), dma((32,)),
        ],
        compiler_params=pltpu.CompilerParams(
            collective_id=0, has_side_effects=True, vmem_limit_bytes=60 * 2**20
        ),
        name="mlp_backward",
    )(
        region_ids.reshape(8, 128),
        positive_phrase.reshape(4, 128),
        block_in,
        block_out,
        phrases,
        hidden_pre.reshape(8, 4, BLK, FL),
        w_in,
        w_out,
    )
    return gi, dwin, dwout


def solution(mesh):
    in_specs = (
        P("col", "row"),
        P("col", "row"),
        P(None, "col"),
        P("row", "col"),
        P("col", "row"),
        P(None, "row"),
        P(),
        P(),
    )
    out_specs = (P("col", "row"), P("row", "col"), P("col", "row"))
    return jax.shard_map(local, mesh=mesh, in_specs=in_specs, out_specs=out_specs, check_vma=False)
```

```python
import jax
import jax.numpy as jnp
from jax import lax
from jax.experimental import pallas as pl
from jax.experimental.pallas import tpu as pltpu
from jax.sharding import PartitionSpec as P

score_scale = 3.0
score_shift = -2.0
epsilon = 1e-06
half_root = 0.7071067811865476
density_norm = 0.3989422804014327

MESH = pl.DeviceIdType.MESH
f32 = jnp.float32
bf16 = jnp.bfloat16
BLK = 32
DL = 384
FL = 768
FH = 384


GROUPS = 4
AWAY = (0, 4, 3, 5, 2, 6, 1, 7)
HOME = AWAY.index(0)
FAR = [AWAY.index(d) for d in (4, 3, 5)]
NEAR = [AWAY.index(d) for d in (1, 7, 2, 6)]


def at(buf, place, part):
    return buf.at[place // 2, part, place % 2]


def nt(a, b):
    return lax.dot_general(a, b, (((1,), (1,)), ((), ())), preferred_element_type=f32)


def nn(a, b):
    return lax.dot_general(a, b, (((1,), (0,)), ((), ())), preferred_element_type=f32)


def tn(a, b):
    return lax.dot_general(a, b, (((0,), (0,)), ((), ())), preferred_element_type=f32)


def split3(v):
    hi = v.astype(bf16)
    rest = v - hi.astype(f32)
    mid = rest.astype(bf16)
    low = (rest - mid.astype(f32)).astype(bf16)
    return jnp.concatenate([hi, mid, low], axis=0)


def kernel(
    ids, pos, bi_own, bo_hbm, ph_hbm, h_hbm, win_hbm, wout_hbm,
    gi_out, dwin_out, dwout_out,
    bo_own, ph, ext, part, corebuf, xs, xr, tot, ag,
    go, bi, win, wout, hv, act, slope, dwout, dwin, dwout_b, dwin_b, pact, pown, pcore, acc, pxs, pxr, ysend, yrecv, gh, pbr, rbuf, gsum,
    lsem, osem, halo_s, halo_r, cs, cr, h7s, h7r, a7s, a7r,
    bis, bir, brs, brr, gos, gor, fas, far, nes, ner, pcs, pcr, pxss, pxsr, yss, ysr, gxs, gxr, gcs, gcr, rs, rr,
):
    r = lax.axis_index("row")
    c = lax.axis_index("col")
    x, yh, k = r // 4, (r // 2) % 2, r % 2
    z, yl = c // 4, c % 4
    ko = 1 - k

    def rdev(xx, yy, kk):
        return (xx * 4 + yy * 2 + kk, c)

    def cdev(cc):
        return (r, cc)

    def rcopy(src, dst, ssem, rsem, dev):
        return pltpu.make_async_remote_copy(
            src_ref=src, dst_ref=dst, send_sem=ssem, recv_sem=rsem,
            device_id=dev, device_id_type=MESH,
        )

    loads = [
        pltpu.make_async_copy(src, dst, lsem.at[n])
        for n, (src, dst) in enumerate(
            ((bo_hbm, bo_own), (bi_own, at(bi, HOME, yl)), (ph_hbm, ph), (wout_hbm, wout), (win_hbm, win))
        )
    ]
    loads += [
        pltpu.make_async_copy(
            h_hbm.at[(z + AWAY[p]) % 8], hv.at[p // 2, :, p % 2], lsem.at[5 + p]
        )
        for p in range(8)
    ]
    for cp in loads:
        cp.start()

    barrier = pltpu.get_barrier_semaphore()
    peers7 = [(dx, dy) for dx in range(4) for dy in range(2) if (dx, dy) != (0, 0)]
    rows = [rdev((x + dx) % 4, (yh + dy) % 2, k) for dx, dy in peers7]
    rows += [rdev((x + dx) % 4, yh, ko) for dx in range(4)]
    for dev in rows:
        pl.semaphore_signal(barrier, inc=1, device_id=dev, device_id_type=MESH)

    def greet(d, _):
        pl.semaphore_signal(
            barrier, inc=1, device_id=cdev((c + d) % 32), device_id_type=MESH
        )
        return 0

    lax.fori_loop(1, 32, greet, 0)
    pl.semaphore_wait(barrier, len(rows) + 31)

    for cp in loads[:2]:
        cp.wait()

    right = rcopy(bo_own, ext.at[pl.ds(0, BLK)], halo_s.at[0], halo_r.at[0], cdev((c + 1) % 32))
    left = rcopy(bo_own, ext.at[pl.ds(2 * BLK, BLK)], halo_s.at[1], halo_r.at[1], cdev((c + 31) % 32))
    right.start()
    left.start()
    ext[pl.ds(BLK, BLK), :] = bo_own[...]
    ext[pl.ds(3 * BLK, BLK), :] = jnp.zeros((BLK, DL), bf16)

    def spread(buf, send, recv, place, to):
        n = place * 4 + to
        slot = at(buf, place, yl)
        return rcopy(slot, slot, send.at[n], recv.at[place * 4 + yl], cdev(z * 4 + to))

    def landed(buf, send, recv, place, of):
        n = place * 4 + of
        slot = at(buf, place, of)
        return rcopy(slot, slot, send.at[n], recv.at[n], cdev(z * 4 + of))

    def each(places, step, every=False):
        for place in places:

            def body(m, _):
                n = (yl + m) % 4
                if every:
                    step(place, n)
                else:

                    @pl.when(n != yl)
                    def _():
                        step(place, n)

                return 0

            lax.fori_loop(0, 4, body, 0)

    def ring(step, back):
        src = AWAY.index(((step - 1) * (7 - 6 * back)) % 8)
        dst = AWAY.index((step * (7 - 6 * back)) % 8)
        half = pl.ds(0, 4) if step < 4 else pl.ds(2 * back, 2)
        n = 2 * step + back
        to = cdev(((z + 1 + 6 * back) % 8) * 4 + yl)
        return rcopy(at(bi, src, half), at(bi, dst, half), brs.at[n - 2], brr.at[n - 2], to)

    def ring_step(step):
        if step == 1:
            each((HOME,), lambda p, n: landed(bi, bis, bir, p, n).wait_recv())
        for back in range(2):
            if step > 1:
                ring(step - 1, back).wait_recv()
            if step < 5:
                ring(step, back).start()

    each((HOME,), lambda p, n: spread(bi, bis, bir, p, n).start())

    lane = lax.broadcasted_iota(jnp.int32, (BLK, 128), 1)
    sub = lax.broadcasted_iota(jnp.int32, (BLK, 128), 0)

    def ids_column(b):
        line = ids[pl.ds(b // 4, 1), :].astype(f32)
        return jnp.sum(jnp.where(lane == (b % 4) * BLK + sub, line, 0.0), axis=1, keepdims=True)

    own_col = ids_column(c)
    line = jnp.where(lane[:1] >= 3 * BLK, -1.0, 0.0)
    for n, b in enumerate(((c + 31) % 32, c, (c + 1) % 32)):
        col = own_col if n == 1 else ids_column(b)
        line += jnp.sum(jnp.where(lane == n * BLK + sub, col, 0.0), axis=0, keepdims=True)
    member = jnp.where(own_col == line, 1.0, 0.0).astype(f32)
    counts = jnp.sum(member, axis=1, keepdims=True)
    pos_col = jnp.zeros((BLK, 1), f32)
    for j in range(4):
        hit = own_col == (lane + j * 128).astype(f32)
        pos_col += jnp.sum(jnp.where(hit, pos[j : j + 1, :].astype(f32), 0.0), axis=1, keepdims=True)

    loads[2].wait()
    right.wait()
    left.wait()
    pooled = nn(member.astype(bf16), ext[...]) / counts
    inner3 = nt(split3(pooled), ph[...])
    inner = inner3[:BLK] + (inner3[BLK : 2 * BLK] + inner3[2 * BLK :])
    squares = jnp.sum(pooled * pooled, axis=1, keepdims=True)
    for j in range(4):
        part[j] = inner[:, j * 128 : (j + 1) * 128]
    part[4] = jnp.broadcast_to(squares, (BLK, 128))

    ring_step(1)

    mine = pl.ds(pl.multiple_of(k * 16, 16), 16)
    theirs = pl.ds(pl.multiple_of(ko * 16, 16), 16)
    cp = rcopy(part.at[:, theirs, :], corebuf, cs, cr, rdev(x, yh, ko))
    cp.start()
    cp.wait()
    for j in range(4):
        xs[j, 0] = part[j, mine, :] + corebuf[j]
        xs[j, 1] = part[4, mine, :] + corebuf[4]
    sends = []
    for i, (dx, dy) in enumerate(peers7):
        xx = (x + dx) % 4
        sends.append(rcopy(xs.at[xx], xr.at[i], h7s.at[i], h7r.at[i], rdev(xx, (yh + dy) % 2, k)))
    for cp in sends:
        cp.start()


    for cp in loads[5:]:
        cp.wait()

    def act_step(n, _):
        g, q, i = n // 8, (n // 2) % 4, n % 2
        v = hv[g, q, i].astype(f32)
        act[g, q, i] = (0.5 * v * (1.0 + lax.erf(v * half_root))).astype(bf16)
        return 0

    lax.fori_loop(0, 16, act_step, 0)
    ring_step(2)

    for cp in sends:
        cp.wait()
    total = xs[x]
    for i in range(7):
        total += xr[i]
    tot[...] = total
    ag[k, x] = total
    sends = []
    for i, (dx, dk) in enumerate(peers7):
        sends.append(
            rcopy(tot, ag.at[k, x], a7s.at[i], a7r.at[i], rdev((x + dx) % 4, yh, (k + dk) % 2))
        )
    for cp in sends:
        cp.start()

    lax.fori_loop(16, 32, act_step, 0)

    def slope_step(n, _):
        v = hv[n // 2, x, n % 2, :, pl.ds(pl.multiple_of(k * FH, 128), FH)].astype(f32)
        slope[n] = 0.5 * (1.0 + lax.erf(v * half_root)) + v * jnp.exp(-0.5 * v * v) * density_norm
        return 0

    lax.fori_loop(0, 8, slope_step, 0)
    ring_step(3)

    for cp in sends:
        cp.wait()

    inner = jnp.concatenate(
        [jnp.concatenate([ag[kk, j, 0] for j in range(4)], axis=1) for kk in range(2)], axis=0
    )
    squares = jnp.concatenate([ag[kk, 0, 1] for kk in range(2)], axis=0)[:, :1]
    width = float(16 * DL)
    norms = jnp.sqrt(squares / width + epsilon)
    scores = inner / norms
    phrase = lax.broadcasted_iota(jnp.int32, (BLK, 512), 1).astype(f32)
    labels = jnp.where(phrase == pos_col, 1.0, -1.0).astype(f32)
    grads = -labels * score_scale * jax.nn.sigmoid(-labels * (score_scale * scores + score_shift))
    pulled3 = nn(split3(grads), ph[...])
    pulled = pulled3[:BLK] + (pulled3[BLK : 2 * BLK] + pulled3[2 * BLK :])
    curve = jnp.sum(grads * scores, axis=1, keepdims=True)
    grad_pooled = pulled / norms - curve * pooled / (width * norms * norms)
    go[HOME // 2, yl, HOME % 2] = (grad_pooled / counts).astype(bf16)

    def to_far(n):
        place = FAR[n]
        dev = cdev(((z + 8 - AWAY[place]) % 8) * 4 + yl)
        return rcopy(at(go, HOME, yl), at(go, place, yl), fas.at[n], far.at[n], dev)

    def to_near(n):
        place = NEAR[n]
        dev = cdev(((z + 8 - AWAY[place]) % 8) * 4 + yl)
        return rcopy(at(go, HOME, pl.ds(0, 4)), at(go, place, pl.ds(0, 4)), nes.at[n], ner.at[n], dev)

    def go_landed(places):
        each(places, lambda p, n: landed(go, gos, gor, p, n).wait_recv())

    def go_spread(places):
        each(places, lambda p, n: spread(go, gos, gor, p, n).start())

    go_spread((HOME,))
    for n in range(3):
        to_far(n).start()
    go_landed((HOME,))
    for n in range(4):
        to_near(n).start()
    for n in range(3):
        to_far(n).wait_recv()
        go_spread(FAR[n : n + 1])

    for cp in loads[3:5]:
        cp.wait()

    whalf = [wout.at[pl.ds(pl.multiple_of(kk * FH, 128), FH), :] for kk in (ko, k)]

    def core_sum(g):
        return rcopy(pact.at[g], pcore.at[g], pcs.at[g], pcr.at[g], rdev(x, yh, ko))

    def x_sum(g, i):
        n = g * 3 + i
        return rcopy(pxs.at[n], pxr.at[n], pxss.at[n], pxsr.at[n], rdev((x + 1 + i) % 4, yh, k))

    def y_sum(g):
        return rcopy(ysend.at[g], yrecv.at[g], yss.at[g], ysr.at[g], rdev(x, 1 - yh, k))

    def x_back(g, i):
        slot = gh.at[k, g, x]
        return rcopy(slot, slot, gxs.at[g * 3 + i], gxr.at[g * 3 + i], rdev((x + 1 + i) % 4, yh, k))

    def x_backed(g, i):
        slot = gh.at[k, g, (x + 3 - i) % 4]
        return rcopy(slot, slot, gxs.at[g * 3 + i], gxr.at[g * 3 + i], rdev((x + 1 + i) % 4, yh, k))

    def core_back(g, q, kk):
        slot = gh.at[kk, g, q]
        return rcopy(slot, slot, gcs.at[g * 4 + q], gcr.at[g * 4 + q], rdev(x, yh, ko))

    def term(place, to):
        n = place * 4
        dev = cdev(((z + AWAY[place]) % 8) * 4 + to)
        return rcopy(at(pbr, place, to), rbuf.at[n + yl], rs.at[n + to], rr.at[n + yl], dev)

    def terms(places, step):
        for place in places:
            each((place,), step, every=place != HOME)

    def product(g):
        for place in (2 * g, 2 * g + 1):
            if place in NEAR:
                to_near(NEAR.index(place)).wait_recv()
            elif place in FAR:
                go_landed((place,))
        a = go[g].reshape(8 * BLK, DL)
        pact[g] = nt(a, whalf[0][...]).astype(bf16).reshape(4, 2, BLK, FH)
        core_sum(g).start()
        pown[g] = nt(a, whalf[1][...]).reshape(4, 2, BLK, FH)

    def to_x(g):
        core_sum(g).wait()
        for i in range(3):
            q = (x + 1 + i) % 4
            pxs[g * 3 + i] = (pown[g, q] + pcore[g, q].astype(f32)).astype(bf16)
            x_sum(g, i).start()
        acc[g] = pown[g, x] + pcore[g, x].astype(f32)

    def to_y(g):
        for i in range(3):
            x_sum(g, i).wait()
        val = acc[g]
        for i in range(3):
            val += pxr[g * 3 + i].astype(f32)
        acc[g] = val
        ysend[g] = val.astype(bf16)
        y_sum(g).start()

    def hidden(g):
        y_sum(g).wait()
        full = acc[g] + yrecv[g].astype(f32)
        gh[k, g, x] = (full * slope[2 * g : 2 * g + 2]).astype(bf16)
        for i in range(3):
            x_back(g, i).start()
        core_back(g, x, k).start()

    def forward(g):
        for i in range(3):
            x_backed(g, i).wait_recv()
            core_back(g, (x + 3 - i) % 4, k).start()

    def branch(g):
        for q in range(4):
            core_back(g, q, ko).wait_recv()
        val = nt(gh[0, g].reshape(8 * BLK, FH), win[:, :FH]) + nt(gh[1, g].reshape(8 * BLK, FH), win[:, FH:])
        pbr[g] = val.astype(bf16).reshape(4, 2, BLK, DL)
        terms((2 * g, 2 * g + 1), lambda p, n: term(p, n).start())

    def weight_out(g):
        val = tn(act[g].reshape(8 * BLK, FL), go[g].reshape(8 * BLK, DL))
        if g:
            val += dwout[...]
        if g < GROUPS - 1:
            dwout[...] = val
        else:
            dwout_b[...] = val.astype(bf16)
            dwout_cp.start()

    def weight_in(g):
        for kk in range(2):
            val = tn(bi[g].reshape(8 * BLK, DL), gh[kk, g].reshape(8 * BLK, FH))
            if g:
                val += dwin[kk]
            if g < GROUPS - 1:
                dwin[kk] = val
            else:
                dwin_b[:, kk * FH : (kk + 1) * FH] = val.astype(bf16)
        if g == GROUPS - 1:
            dwin_cp.start()

    dwout_cp = pltpu.make_async_copy(dwout_b, dwout_out, osem.at[0])
    dwin_cp = pltpu.make_async_copy(dwin_b, dwin_out, osem.at[1])

    steps = (branch, forward, hidden, to_y, to_x, product)
    for t in range(GROUPS + len(steps) - 1):
        for late, step in enumerate(steps):
            g = t - (len(steps) - 1 - late)
            if 0 <= g < GROUPS:
                step(g)
        if 0 <= t - 1 < GROUPS:
            weight_out(t - 1)
        if t == 1:
            ring_step(4)
        if t == GROUPS:
            ring_step(5)
        if 0 <= t - 5 < GROUPS:
            weight_in(t - 5)

    gsum[...] = go[HOME // 2, yl, HOME % 2].astype(f32) + pbr[HOME // 2, yl, HOME % 2].astype(f32)

    def collect(place, of):
        n = place * 4 + of
        slot = rbuf.at[n]
        rcopy(slot, slot, rs.at[n], rr.at[n], cdev((c + 1) % 32)).wait_recv()
        gsum[...] += rbuf[n].astype(f32)

    terms(range(8), collect)
    gi_out[...] = gsum[...].astype(bf16)

    for g in range(GROUPS):
        for i in range(3):
            x_back(g, i).wait_send()
        for q in range(4):
            core_back(g, q, k).wait_send()

    terms(range(8), lambda p, n: term(p, n).wait_send())
    each([HOME] + FAR, lambda p, n: spread(go, gos, gor, p, n).wait_send())
    for n in range(3):
        to_far(n).wait_send()
    for n in range(4):
        to_near(n).wait_send()
    each((HOME,), lambda p, n: spread(bi, bis, bir, p, n).wait_send())
    for step in range(1, 5):
        for back in range(2):
            ring(step, back).wait_send()
    dwout_cp.wait()
    dwin_cp.wait()


def local(block_in, block_out, hidden_pre, w_in, w_out, phrases, region_ids, positive_phrase):
    dma = pltpu.SemaphoreType.DMA
    vm = pltpu.VMEM
    vspec = pl.BlockSpec(memory_space=pltpu.VMEM)
    hspec = pl.BlockSpec(memory_space=pltpu.HBM)
    gi, dwin, dwout = pl.pallas_call(
        kernel,
        out_shape=(
            jax.ShapeDtypeStruct((BLK, DL), bf16),
            jax.ShapeDtypeStruct((DL, FL), bf16),
            jax.ShapeDtypeStruct((FL, DL), bf16),
        ),
        in_specs=[vspec] * 2 + [hspec] * 6,
        out_specs=(vspec, hspec, hspec),
        scratch_shapes=[
            vm((BLK, DL), bf16),
            vm((512, DL), bf16),
            vm((4 * BLK, DL), bf16),
            vm((5, BLK, 128), f32),
            vm((5, 16, 128), f32),
            vm((4, 2, 16, 128), f32),
            vm((7, 2, 16, 128), f32),
            vm((2, 16, 128), f32),
            vm((2, 4, 2, 16, 128), f32),
            vm((4, 4, 2, BLK, DL), bf16),
            vm((4, 4, 2, BLK, DL), bf16),
            vm((DL, FL), bf16),
            vm((FL, DL), bf16),
            vm((4, 4, 2, BLK, FL), bf16),
            vm((4, 4, 2, BLK, FL), bf16),
            vm((8, BLK, FH), f32),
            vm((FL, DL), f32),
            vm((2, DL, FH), f32),
            vm((FL, DL), bf16),
            vm((DL, FL), bf16),
            vm((4, 4, 2, BLK, FH), bf16),
            vm((4, 4, 2, BLK, FH), f32),
            vm((4, 4, 2, BLK, FH), bf16),
            vm((4, 2, BLK, FH), f32),
            vm((12, 2, BLK, FH), bf16),
            vm((12, 2, BLK, FH), bf16),
            vm((4, 2, BLK, FH), bf16),
            vm((4, 2, BLK, FH), bf16),
            vm((2, 4, 4, 2, BLK, FH), bf16),
            vm((4, 4, 2, BLK, DL), bf16),
            vm((32, BLK, DL), bf16),
            vm((BLK, DL), f32),
            dma((13,)), dma((2,)), dma((2,)), dma((2,)), dma, dma, dma((7,)), dma((7,)), dma((7,)), dma((7,)),
            dma((32,)), dma((32,)), dma((8,)), dma((8,)), dma((32,)), dma((32,)), dma((3,)), dma((3,)), dma((4,)), dma((4,)),
            dma((4,)), dma((4,)), dma((12,)), dma((12,)), dma((4,)), dma((4,)),
            dma((12,)), dma((12,)), dma((16,)), dma((16,)), dma((32,)), dma((32,)),
        ],
        compiler_params=pltpu.CompilerParams(
            collective_id=0, has_side_effects=True, vmem_limit_bytes=60 * 2**20
        ),
        name="mlp_backward",
    )(
        region_ids.reshape(8, 128),
        positive_phrase.reshape(4, 128),
        block_in,
        block_out,
        phrases,
        hidden_pre.reshape(8, 4, BLK, FL),
        w_in,
        w_out,
    )
    return gi, dwin, dwout


def solution(mesh):
    in_specs = (
        P("col", "row"),
        P("col", "row"),
        P(None, "col"),
        P("row", "col"),
        P("col", "row"),
        P(None, "row"),
        P(),
        P(),
    )
    out_specs = (P("col", "row"), P("row", "col"), P("col", "row"))
    return jax.shard_map(local, mesh=mesh, in_specs=in_specs, out_specs=out_specs, check_vma=False)
```

```python
import jax
import jax.numpy as jnp
from jax import lax
from jax.experimental import pallas as pl
from jax.experimental.pallas import tpu as pltpu
from jax.sharding import PartitionSpec as P

score_scale = 3.0
score_shift = -2.0
epsilon = 1e-06
half_root = 0.7071067811865476
density_norm = 0.3989422804014327

MESH = pl.DeviceIdType.MESH
f32 = jnp.float32
bf16 = jnp.bfloat16
BLK = 32
DL = 384
FL = 768
FH = 384


GROUPS = 4
AWAY = (0, 4, 2, 6, 3, 5, 1, 7)
HOME = AWAY.index(0)
FAR = [AWAY.index(d) for d in (4, 3, 5)]
NEAR = [AWAY.index(d) for d in (2, 6, 1, 7)]


def at(buf, place, part):
    return buf.at[place // 2, part, place % 2]


def nt(a, b):
    return lax.dot_general(a, b, (((1,), (1,)), ((), ())), preferred_element_type=f32)


def nn(a, b):
    return lax.dot_general(a, b, (((1,), (0,)), ((), ())), preferred_element_type=f32)


def tn(a, b):
    return lax.dot_general(a, b, (((0,), (0,)), ((), ())), preferred_element_type=f32)


def split3(v):
    hi = v.astype(bf16)
    rest = v - hi.astype(f32)
    mid = rest.astype(bf16)
    low = (rest - mid.astype(f32)).astype(bf16)
    return jnp.concatenate([hi, mid, low], axis=0)


def kernel(
    ids, pos, bi_own, bo_hbm, ph_hbm, h_hbm, win_hbm, wout_hbm,
    gi_out, dwin_out, dwout_out,
    bo_own, ph, ext, part, corebuf, xs, xr, tot, ag,
    go, bi, win, wout, hv, act, slope, dwout, dwin, dwout_b, dwin_b, pact, pown, pcore, acc, pxs, pxr, ysend, yrecv, gh, pbr, rbuf, gsum,
    lsem, osem, halo_s, halo_r, cs, cr, h7s, h7r, a7s, a7r,
    bis, bir, brs, brr, gos, gor, fas, far, nes, ner, pcs, pcr, pxss, pxsr, yss, ysr, gxs, gxr, gcs, gcr, rs, rr,
):
    r = lax.axis_index("row")
    c = lax.axis_index("col")
    x, yh, k = r // 4, (r // 2) % 2, r % 2
    z, yl = c // 4, c % 4
    ko = 1 - k

    def rdev(xx, yy, kk):
        return (xx * 4 + yy * 2 + kk, c)

    def cdev(cc):
        return (r, cc)

    def rcopy(src, dst, ssem, rsem, dev):
        return pltpu.make_async_remote_copy(
            src_ref=src, dst_ref=dst, send_sem=ssem, recv_sem=rsem,
            device_id=dev, device_id_type=MESH,
        )

    loads = [
        pltpu.make_async_copy(src, dst, lsem.at[n])
        for n, (src, dst) in enumerate(
            ((bo_hbm, bo_own), (bi_own, at(bi, HOME, yl)), (ph_hbm, ph), (wout_hbm, wout), (win_hbm, win))
        )
    ]
    loads += [
        pltpu.make_async_copy(
            h_hbm.at[(z + AWAY[p]) % 8], hv.at[p // 2, :, p % 2], lsem.at[5 + p]
        )
        for p in range(8)
    ]
    for cp in loads:
        cp.start()

    barrier = pltpu.get_barrier_semaphore()
    peers7 = [(dx, dy) for dx in range(4) for dy in range(2) if (dx, dy) != (0, 0)]
    rows = [rdev((x + dx) % 4, (yh + dy) % 2, k) for dx, dy in peers7]
    rows += [rdev((x + dx) % 4, yh, ko) for dx in range(4)]
    for dev in rows:
        pl.semaphore_signal(barrier, inc=1, device_id=dev, device_id_type=MESH)

    def greet(d, _):
        pl.semaphore_signal(
            barrier, inc=1, device_id=cdev((c + d) % 32), device_id_type=MESH
        )
        return 0

    lax.fori_loop(1, 32, greet, 0)
    pl.semaphore_wait(barrier, len(rows) + 31)

    for cp in loads[:2]:
        cp.wait()

    right = rcopy(bo_own, ext.at[pl.ds(0, BLK)], halo_s.at[0], halo_r.at[0], cdev((c + 1) % 32))
    left = rcopy(bo_own, ext.at[pl.ds(2 * BLK, BLK)], halo_s.at[1], halo_r.at[1], cdev((c + 31) % 32))
    right.start()
    left.start()
    ext[pl.ds(BLK, BLK), :] = bo_own[...]
    ext[pl.ds(3 * BLK, BLK), :] = jnp.zeros((BLK, DL), bf16)

    def spread(buf, send, recv, place, to):
        n = place * 4 + to
        slot = at(buf, place, yl)
        return rcopy(slot, slot, send.at[n], recv.at[place * 4 + yl], cdev(z * 4 + to))

    def landed(buf, send, recv, place, of):
        n = place * 4 + of
        slot = at(buf, place, of)
        return rcopy(slot, slot, send.at[n], recv.at[n], cdev(z * 4 + of))

    def each(places, step, every=False):
        for place in places:

            def body(m, _):
                n = (yl + m) % 4
                if every:
                    step(place, n)
                else:

                    @pl.when(n != yl)
                    def _():
                        step(place, n)

                return 0

            lax.fori_loop(0, 4, body, 0)

    def ring(step, back):
        src = AWAY.index(((step - 1) * (7 - 6 * back)) % 8)
        dst = AWAY.index((step * (7 - 6 * back)) % 8)
        half = pl.ds(0, 4) if step < 4 else pl.ds(2 * back, 2)
        n = 2 * step + back
        to = cdev(((z + 1 + 6 * back) % 8) * 4 + yl)
        return rcopy(at(bi, src, half), at(bi, dst, half), brs.at[n - 2], brr.at[n - 2], to)

    def ring_step(step):
        if step == 1:
            each((HOME,), lambda p, n: landed(bi, bis, bir, p, n).wait_recv())
        for back in range(2):
            if step > 1:
                ring(step - 1, back).wait_recv()
            if step < 5:
                ring(step, back).start()

    each((HOME,), lambda p, n: spread(bi, bis, bir, p, n).start())

    lane = lax.broadcasted_iota(jnp.int32, (BLK, 128), 1)
    sub = lax.broadcasted_iota(jnp.int32, (BLK, 128), 0)

    def ids_column(b):
        line = ids[pl.ds(b // 4, 1), :].astype(f32)
        return jnp.sum(jnp.where(lane == (b % 4) * BLK + sub, line, 0.0), axis=1, keepdims=True)

    own_col = ids_column(c)
    line = jnp.where(lane[:1] >= 3 * BLK, -1.0, 0.0)
    for n, b in enumerate(((c + 31) % 32, c, (c + 1) % 32)):
        col = own_col if n == 1 else ids_column(b)
        line += jnp.sum(jnp.where(lane == n * BLK + sub, col, 0.0), axis=0, keepdims=True)
    member = jnp.where(own_col == line, 1.0, 0.0).astype(f32)
    counts = jnp.sum(member, axis=1, keepdims=True)
    pos_col = jnp.zeros((BLK, 1), f32)
    for j in range(4):
        hit = own_col == (lane + j * 128).astype(f32)
        pos_col += jnp.sum(jnp.where(hit, pos[j : j + 1, :].astype(f32), 0.0), axis=1, keepdims=True)

    loads[2].wait()
    right.wait()
    left.wait()
    pooled = nn(member.astype(bf16), ext[...]) / counts
    inner3 = nt(split3(pooled), ph[...])
    inner = inner3[:BLK] + (inner3[BLK : 2 * BLK] + inner3[2 * BLK :])
    squares = jnp.sum(pooled * pooled, axis=1, keepdims=True)
    for j in range(4):
        part[j] = inner[:, j * 128 : (j + 1) * 128]
    part[4] = jnp.broadcast_to(squares, (BLK, 128))

    ring_step(1)

    mine = pl.ds(pl.multiple_of(k * 16, 16), 16)
    theirs = pl.ds(pl.multiple_of(ko * 16, 16), 16)
    cp = rcopy(part.at[:, theirs, :], corebuf, cs, cr, rdev(x, yh, ko))
    cp.start()
    cp.wait()
    for j in range(4):
        xs[j, 0] = part[j, mine, :] + corebuf[j]
        xs[j, 1] = part[4, mine, :] + corebuf[4]
    sends = []
    for i, (dx, dy) in enumerate(peers7):
        xx = (x + dx) % 4
        sends.append(rcopy(xs.at[xx], xr.at[i], h7s.at[i], h7r.at[i], rdev(xx, (yh + dy) % 2, k)))
    for cp in sends:
        cp.start()


    for cp in loads[5:]:
        cp.wait()

    def act_step(n, _):
        g, q, i = n // 8, (n // 2) % 4, n % 2
        v = hv[g, q, i].astype(f32)
        act[g, q, i] = (0.5 * v * (1.0 + lax.erf(v * half_root))).astype(bf16)
        return 0

    lax.fori_loop(0, 16, act_step, 0)
    ring_step(2)

    for cp in sends:
        cp.wait()
    total = xs[x]
    for i in range(7):
        total += xr[i]
    tot[...] = total
    ag[k, x] = total
    sends = []
    for i, (dx, dk) in enumerate(peers7):
        sends.append(
            rcopy(tot, ag.at[k, x], a7s.at[i], a7r.at[i], rdev((x + dx) % 4, yh, (k + dk) % 2))
        )
    for cp in sends:
        cp.start()

    lax.fori_loop(16, 32, act_step, 0)

    def slope_step(n, _):
        v = hv[n // 2, x, n % 2, :, pl.ds(pl.multiple_of(k * FH, 128), FH)].astype(f32)
        slope[n] = 0.5 * (1.0 + lax.erf(v * half_root)) + v * jnp.exp(-0.5 * v * v) * density_norm
        return 0

    lax.fori_loop(0, 8, slope_step, 0)
    ring_step(3)

    for cp in sends:
        cp.wait()

    inner = jnp.concatenate(
        [jnp.concatenate([ag[kk, j, 0] for j in range(4)], axis=1) for kk in range(2)], axis=0
    )
    squares = jnp.concatenate([ag[kk, 0, 1] for kk in range(2)], axis=0)[:, :1]
    width = float(16 * DL)
    norms = jnp.sqrt(squares / width + epsilon)
    scores = inner / norms
    phrase = lax.broadcasted_iota(jnp.int32, (BLK, 512), 1).astype(f32)
    labels = jnp.where(phrase == pos_col, 1.0, -1.0).astype(f32)
    grads = -labels * score_scale * jax.nn.sigmoid(-labels * (score_scale * scores + score_shift))
    pulled3 = nn(split3(grads), ph[...])
    pulled = pulled3[:BLK] + (pulled3[BLK : 2 * BLK] + pulled3[2 * BLK :])
    curve = jnp.sum(grads * scores, axis=1, keepdims=True)
    grad_pooled = pulled / norms - curve * pooled / (width * norms * norms)
    go[HOME // 2, yl, HOME % 2] = (grad_pooled / counts).astype(bf16)

    def to_far(n):
        place = FAR[n]
        dev = cdev(((z + 8 - AWAY[place]) % 8) * 4 + yl)
        return rcopy(at(go, HOME, yl), at(go, place, yl), fas.at[n], far.at[n], dev)

    def to_near(n):
        place = NEAR[n]
        dev = cdev(((z + 8 - AWAY[place]) % 8) * 4 + yl)
        return rcopy(at(go, HOME, pl.ds(0, 4)), at(go, place, pl.ds(0, 4)), nes.at[n], ner.at[n], dev)

    def go_landed(places):
        each(places, lambda p, n: landed(go, gos, gor, p, n).wait_recv())

    def go_spread(places):
        each(places, lambda p, n: spread(go, gos, gor, p, n).start())

    go_spread((HOME,))
    for n in range(3):
        to_far(n).start()
    go_landed((HOME,))
    for n in range(4):
        to_near(n).start()
    for n in range(3):
        to_far(n).wait_recv()
        go_spread(FAR[n : n + 1])

    for cp in loads[3:5]:
        cp.wait()

    whalf = [wout.at[pl.ds(pl.multiple_of(kk * FH, 128), FH), :] for kk in (ko, k)]

    def core_sum(g):
        return rcopy(pact.at[g], pcore.at[g], pcs.at[g], pcr.at[g], rdev(x, yh, ko))

    def x_sum(g, i):
        n = g * 3 + i
        return rcopy(pxs.at[n], pxr.at[n], pxss.at[n], pxsr.at[n], rdev((x + 1 + i) % 4, yh, k))

    def y_sum(g):
        return rcopy(ysend.at[g], yrecv.at[g], yss.at[g], ysr.at[g], rdev(x, 1 - yh, k))

    def x_back(g, i):
        slot = gh.at[k, g, x]
        return rcopy(slot, slot, gxs.at[g * 3 + i], gxr.at[g * 3 + i], rdev((x + 1 + i) % 4, yh, k))

    def x_backed(g, i):
        slot = gh.at[k, g, (x + 3 - i) % 4]
        return rcopy(slot, slot, gxs.at[g * 3 + i], gxr.at[g * 3 + i], rdev((x + 1 + i) % 4, yh, k))

    def core_back(g, q, kk):
        slot = gh.at[kk, g, q]
        return rcopy(slot, slot, gcs.at[g * 4 + q], gcr.at[g * 4 + q], rdev(x, yh, ko))

    def term(place, to):
        n = place * 4
        dev = cdev(((z + AWAY[place]) % 8) * 4 + to)
        return rcopy(at(pbr, place, to), rbuf.at[n + yl], rs.at[n + to], rr.at[n + yl], dev)

    def terms(places, step):
        for place in places:
            each((place,), step, every=place != HOME)

    def product(g):
        for place in (2 * g, 2 * g + 1):
            if place in NEAR:
                to_near(NEAR.index(place)).wait_recv()
            elif place in FAR:
                go_landed((place,))
        a = go[g].reshape(8 * BLK, DL)
        pact[g] = nt(a, whalf[0][...]).astype(bf16).reshape(4, 2, BLK, FH)
        core_sum(g).start()
        pown[g] = nt(a, whalf[1][...]).reshape(4, 2, BLK, FH)

    def to_x(g):
        core_sum(g).wait()
        for i in range(3):
            q = (x + 1 + i) % 4
            pxs[g * 3 + i] = (pown[g, q] + pcore[g, q].astype(f32)).astype(bf16)
            x_sum(g, i).start()
        acc[g] = pown[g, x] + pcore[g, x].astype(f32)

    def to_y(g):
        for i in range(3):
            x_sum(g, i).wait()
        val = acc[g]
        for i in range(3):
            val += pxr[g * 3 + i].astype(f32)
        acc[g] = val
        ysend[g] = val.astype(bf16)
        y_sum(g).start()

    def hidden(g):
        y_sum(g).wait()
        full = acc[g] + yrecv[g].astype(f32)
        gh[k, g, x] = (full * slope[2 * g : 2 * g + 2]).astype(bf16)
        for i in range(3):
            x_back(g, i).start()
        core_back(g, x, k).start()

    def forward(g):
        for i in range(3):
            x_backed(g, i).wait_recv()
            core_back(g, (x + 3 - i) % 4, k).start()

    def branch(g):
        for q in range(4):
            core_back(g, q, ko).wait_recv()
        val = nt(gh[0, g].reshape(8 * BLK, FH), win[:, :FH]) + nt(gh[1, g].reshape(8 * BLK, FH), win[:, FH:])
        pbr[g] = val.astype(bf16).reshape(4, 2, BLK, DL)
        terms((2 * g, 2 * g + 1), lambda p, n: term(p, n).start())

    def weight_out(g):
        val = tn(act[g].reshape(8 * BLK, FL), go[g].reshape(8 * BLK, DL))
        if g:
            val += dwout[...]
        if g < GROUPS - 1:
            dwout[...] = val
        else:
            dwout_b[...] = val.astype(bf16)
            dwout_cp.start()

    def weight_in(g):
        for kk in range(2):
            val = tn(bi[g].reshape(8 * BLK, DL), gh[kk, g].reshape(8 * BLK, FH))
            if g:
                val += dwin[kk]
            if g < GROUPS - 1:
                dwin[kk] = val
            else:
                dwin_b[:, kk * FH : (kk + 1) * FH] = val.astype(bf16)
        if g == GROUPS - 1:
            dwin_cp.start()

    dwout_cp = pltpu.make_async_copy(dwout_b, dwout_out, osem.at[0])
    dwin_cp = pltpu.make_async_copy(dwin_b, dwin_out, osem.at[1])

    steps = (branch, forward, hidden, to_y, to_x, product)
    for t in range(GROUPS + len(steps) - 1):
        for late, step in enumerate(steps):
            g = t - (len(steps) - 1 - late)
            if 0 <= g < GROUPS:
                step(g)
        if 0 <= t - 1 < GROUPS:
            weight_out(t - 1)
        if t == 1:
            ring_step(4)
        if t == GROUPS:
            ring_step(5)
        if 0 <= t - 5 < GROUPS:
            weight_in(t - 5)

    gsum[...] = go[HOME // 2, yl, HOME % 2].astype(f32) + pbr[HOME // 2, yl, HOME % 2].astype(f32)

    def collect(place, of):
        n = place * 4 + of
        slot = rbuf.at[n]
        rcopy(slot, slot, rs.at[n], rr.at[n], cdev((c + 1) % 32)).wait_recv()
        gsum[...] += rbuf[n].astype(f32)

    terms(range(8), collect)
    gi_out[...] = gsum[...].astype(bf16)

    for g in range(GROUPS):
        for i in range(3):
            x_back(g, i).wait_send()
        for q in range(4):
            core_back(g, q, k).wait_send()

    terms(range(8), lambda p, n: term(p, n).wait_send())
    each([HOME] + FAR, lambda p, n: spread(go, gos, gor, p, n).wait_send())
    for n in range(3):
        to_far(n).wait_send()
    for n in range(4):
        to_near(n).wait_send()
    each((HOME,), lambda p, n: spread(bi, bis, bir, p, n).wait_send())
    for step in range(1, 5):
        for back in range(2):
            ring(step, back).wait_send()
    dwout_cp.wait()
    dwin_cp.wait()


def local(block_in, block_out, hidden_pre, w_in, w_out, phrases, region_ids, positive_phrase):
    dma = pltpu.SemaphoreType.DMA
    vm = pltpu.VMEM
    vspec = pl.BlockSpec(memory_space=pltpu.VMEM)
    hspec = pl.BlockSpec(memory_space=pltpu.HBM)
    gi, dwin, dwout = pl.pallas_call(
        kernel,
        out_shape=(
            jax.ShapeDtypeStruct((BLK, DL), bf16),
            jax.ShapeDtypeStruct((DL, FL), bf16),
            jax.ShapeDtypeStruct((FL, DL), bf16),
        ),
        in_specs=[vspec] * 2 + [hspec] * 6,
        out_specs=(vspec, hspec, hspec),
        scratch_shapes=[
            vm((BLK, DL), bf16),
            vm((512, DL), bf16),
            vm((4 * BLK, DL), bf16),
            vm((5, BLK, 128), f32),
            vm((5, 16, 128), f32),
            vm((4, 2, 16, 128), f32),
            vm((7, 2, 16, 128), f32),
            vm((2, 16, 128), f32),
            vm((2, 4, 2, 16, 128), f32),
            vm((4, 4, 2, BLK, DL), bf16),
            vm((4, 4, 2, BLK, DL), bf16),
            vm((DL, FL), bf16),
            vm((FL, DL), bf16),
            vm((4, 4, 2, BLK, FL), bf16),
            vm((4, 4, 2, BLK, FL), bf16),
            vm((8, BLK, FH), f32),
            vm((FL, DL), f32),
            vm((2, DL, FH), f32),
            vm((FL, DL), bf16),
            vm((DL, FL), bf16),
            vm((4, 4, 2, BLK, FH), bf16),
            vm((4, 4, 2, BLK, FH), f32),
            vm((4, 4, 2, BLK, FH), bf16),
            vm((4, 2, BLK, FH), f32),
            vm((12, 2, BLK, FH), bf16),
            vm((12, 2, BLK, FH), bf16),
            vm((4, 2, BLK, FH), bf16),
            vm((4, 2, BLK, FH), bf16),
            vm((2, 4, 4, 2, BLK, FH), bf16),
            vm((4, 4, 2, BLK, DL), bf16),
            vm((32, BLK, DL), bf16),
            vm((BLK, DL), f32),
            dma((13,)), dma((2,)), dma((2,)), dma((2,)), dma, dma, dma((7,)), dma((7,)), dma((7,)), dma((7,)),
            dma((32,)), dma((32,)), dma((8,)), dma((8,)), dma((32,)), dma((32,)), dma((3,)), dma((3,)), dma((4,)), dma((4,)),
            dma((4,)), dma((4,)), dma((12,)), dma((12,)), dma((4,)), dma((4,)),
            dma((12,)), dma((12,)), dma((16,)), dma((16,)), dma((32,)), dma((32,)),
        ],
        compiler_params=pltpu.CompilerParams(
            collective_id=0, has_side_effects=True, vmem_limit_bytes=60 * 2**20
        ),
        name="mlp_backward",
    )(
        region_ids.reshape(8, 128),
        positive_phrase.reshape(4, 128),
        block_in,
        block_out,
        phrases,
        hidden_pre.reshape(8, 4, BLK, FL),
        w_in,
        w_out,
    )
    return gi, dwin, dwout


def solution(mesh):
    in_specs = (
        P("col", "row"),
        P("col", "row"),
        P(None, "col"),
        P("row", "col"),
        P("col", "row"),
        P(None, "row"),
        P(),
        P(),
    )
    out_specs = (P("col", "row"), P("row", "col"), P("col", "row"))
    return jax.shard_map(local, mesh=mesh, in_specs=in_specs, out_specs=out_specs, check_vma=False)
```
